128 devices in a mesh: inner: 8 (over x, z_hi), cols: 16 (over y, z_lo, core).
Axes of the slice: x: 4, y: 4, z: 4 (z_hi: 2, z_lo: 2; z = z_hi * 2 + z_lo), core: 2. Of those that a mesh axis runs over, the one named last changes fastest.
Arguments:
- x_tiles: float32 [64, 64, 128, 128], P('inner', 'cols'), may hold values from -4 to 4
- tile_col: int32 [64, 64], P('inner', 'cols'), may hold values from 0 to 959, as said below
- keep_mask: int32 [64, 64, 64], P('inner', None, 'cols'), may hold values 0 or 1
- out_rows: int32 [128], P(('inner', 'cols')), may hold values from 0 to 959, as said below
- out_cols: int32 [128], P(('inner', 'cols')), may hold values from 0 to 959, as said below
Outputs:
- product_tiles: float32 [128, 128, 128], P(('inner', 'cols'))
The draws below stay inside these ranges and needn't reach their ends.
Inputs may be any that keep to these rules, and one draw needn't show every extreme that they name: `tile_col`: within block row k, the 4 entries of column slice c (positions c * 4 to c * 4 + 3) are distinct block columns of c * 60 to c * 60 + 59. `out_cols`: slot s names a block column of column slice (s) % 16 that is stored in some block row. `out_rows`: each slot's block row is stored in some block row together with the slot's block column. The slots of one column slice name block rows that lie in distinct column slices. A slot's two block columns may be stored together in any number of block rows of every index of inner, up to all 8 block rows of one index, and in every draw some slot's are stored together in all 8 block rows of some index.
All inputs are finite; a program needn't handle non-finite values. No bound on the sum of `keep_mask` on one device may be relied on, other than what follows from the above.
Results may differ from the reference program's by a relative error of at most 0.0003.
Values sent between devices are 32-bit elements; how exact they have to be, the bound alone decides.
A program may use at most 128 MiB of HBM per device.

```python
import jax
import jax.numpy as jnp
from jax import lax

BLK = 128
KB_DEV = 8
RPK = 4
JB_DEV = 60
OT_DEV = 1
KB = 64
SLOTS = 128
N_INNER = 8
N_COLS = 16


def column_table(key):
    root = jax.random.randint(jax.random.fold_in(key, 5), (KB, N_COLS, 1), 0, JB_DEV)
    stride = jax.random.randint(jax.random.fold_in(key, 6), (KB, N_COLS, 1), 1, JB_DEV // RPK + 1)
    offsets = jnp.arange(RPK, dtype=jnp.int32)[None, None, :]
    own_within = ((root + offsets * stride) % JB_DEV).reshape(N_INNER, KB_DEV, N_COLS, RPK)
    base_root = jax.random.randint(jax.random.fold_in(key, 7), (1, 1, N_COLS, 1), 0, JB_DEV)
    base_stride = jax.random.randint(jax.random.fold_in(key, 8), (1, 1, N_COLS, 1), 1, JB_DEV // RPK + 1)
    base_within = (base_root + offsets[None] * base_stride) % JB_DEV
    copy_draw = jax.random.randint(jax.random.fold_in(key, 9), (N_INNER, KB_DEV), 0, 2)
    anchor = jax.random.randint(jax.random.fold_in(key, 10), (N_INNER,), 0, KB_DEV).astype(jnp.int32)
    full = jax.random.randint(jax.random.fold_in(key, 12), (), 0, N_INNER).astype(jnp.int32)
    anchor_hot = jnp.arange(KB_DEV, dtype=jnp.int32)[None, :] == anchor[:, None]
    full_hot = (jnp.arange(N_INNER, dtype=jnp.int32) == full)[:, None]
    copied = (copy_draw == 1) | anchor_hot | full_hot
    within = jnp.where(copied[:, :, None, None], base_within, own_within)
    within = within.reshape(KB, N_COLS, RPK)
    base = (jnp.arange(N_COLS, dtype=jnp.int32) * JB_DEV)[None, :, None]
    table = (base + within).reshape(KB, N_COLS * RPK).astype(jnp.int32)
    return (table, anchor, full)


def slot_pairs(key):
    table, anchor, full = column_table(key)
    slot_key = jax.random.fold_in(key, 11)
    slot_index = jnp.arange(SLOTS, dtype=jnp.int32)
    column_slice = slot_index // OT_DEV % N_COLS
    rank = slot_index // (OT_DEV * N_COLS) * OT_DEV + slot_index % OT_DEV
    order_keys = jax.random.split(jax.random.fold_in(slot_key, 4), N_COLS)
    orders = jax.vmap(lambda k: jax.random.permutation(k, N_COLS))(order_keys).astype(jnp.int32)
    left_slice = orders[column_slice, rank]
    shard_pick = jax.random.randint(jax.random.fold_in(slot_key, 1), (SLOTS,), 0, N_INNER).astype(jnp.int32)
    shard_pick = jnp.where(slot_index == 0, full, shard_pick)
    row_pick = shard_pick * KB_DEV + anchor[shard_pick]
    right_pick = jax.random.randint(jax.random.fold_in(slot_key, 2), (SLOTS,), 0, RPK)
    left_pick = jax.random.randint(jax.random.fold_in(slot_key, 3), (SLOTS,), 0, RPK)
    picked = table[row_pick]
    right_col = jnp.take_along_axis(picked, (column_slice * RPK + right_pick)[:, None], axis=1)[:, 0]
    left_col = jnp.take_along_axis(picked, (left_slice * RPK + left_pick)[:, None], axis=1)[:, 0]
    return (left_col.astype(jnp.int32), right_col.astype(jnp.int32))


def draw_tile_col(key, part):
    table, anchor, full = column_table(key)
    return table


def draw_out_rows(key, part):
    left_col, right_col = slot_pairs(key)
    return left_col


def draw_out_cols(key, part):
    left_col, right_col = slot_pairs(key)
    return right_col


def with_ends(result, stream_key, low, top_value):
    longest = result.shape.index(max(result.shape))
    spots = []
    for shift in (0, 1):
        where = [jax.random.randint(jax.random.fold_in(stream_key, axis), (), 0, length) for axis, length in enumerate(result.shape)]
        where[longest] = (where[longest] + shift) % result.shape[longest]
        spots.append(tuple(where))
    return result.at[spots[0]].set(low).at[spots[1]].set(top_value)


def shard_levels(stream_key, dims, pieces, smallest, top_value):
    factor_of, own = 1.0, jax.random.fold_in(stream_key, 6)
    for dim, shards_of in pieces:
        steps = jnp.exp(jax.random.uniform(jax.random.fold_in(own, dim), (shards_of,), jnp.float32, smallest / len(pieces), top_value / len(pieces)))
        factor_of = factor_of * jnp.repeat(steps, dims[dim] // shards_of).reshape([-1 if axis == dim else 1 for axis in range(len(dims))])
    return factor_of


def scatter_about(stream_key, shape, deviation, most, pieces=(), kind=jnp.bfloat16):
    level = shard_levels(stream_key, shape, pieces, -0.22, 0.18) if pieces else 1.0
    entries = jax.random.normal(stream_key, shape, jnp.float32) * deviation * level
    return jnp.minimum(jnp.maximum(entries, -most), most).astype(kind)


def setup_inputs(seed: int = 0) -> dict:
    arg_keys = jax.random.split(jax.random.key(seed), 6)
    x_tiles = scatter_about(arg_keys[0], (KB, N_COLS * RPK, BLK, BLK), (BLK ** -0.25), 4.0, ((0, 8), (1, 16)), jnp.float32)
    tile_col = draw_tile_col(jax.random.fold_in(arg_keys[5], 71), 0)
    keep_mask = with_ends((jax.random.randint(arg_keys[2], (KB, N_COLS * RPK, N_COLS * RPK), 0, 8) < 7).astype(jnp.int32), jax.random.fold_in(arg_keys[2], 1), 0, 1)
    out_rows = draw_out_rows(jax.random.fold_in(arg_keys[5], 71), 0)
    out_cols = draw_out_cols(jax.random.fold_in(arg_keys[5], 71), 0)
    return {"x_tiles": x_tiles, "tile_col": tile_col, "keep_mask": keep_mask, "out_rows": out_rows, "out_cols": out_cols}


def row_term(tiles, columns, keep, out_rows, out_cols):
    pick_left = (columns[None, :] == out_rows[:, None]).astype(jnp.float32)
    pick_right = (columns[None, :] == out_cols[:, None]).astype(jnp.float32)
    high = lax.Precision.HIGHEST
    left = jnp.einsum("sp,pab->sab", pick_left, tiles, precision=high)
    right = jnp.einsum("sq,qab->sab", pick_right, tiles, precision=high)
    gate = jnp.einsum("sp,pq,sq->s", pick_left, keep.astype(jnp.float32), pick_right, precision=high)
    return gate[:, None, None] * jnp.einsum("sab,sac->sbc", left, right, precision=high)


def reference(x_tiles, tile_col, keep_mask, out_rows, out_cols):
    start = jnp.zeros((out_rows.shape[0], x_tiles.shape[2], x_tiles.shape[3]), jnp.float32)

    def step(total, row):
        tiles, columns, keep = row
        return total + row_term(tiles, columns, keep, out_rows, out_cols), None

    total, unused = lax.scan(step, start, (x_tiles, tile_col, keep_mask))
    return total
```

```python
import jax
import jax.numpy as jnp
from jax import lax
from jax.experimental import pallas as pl
from jax.experimental.pallas import tpu as pltpu
from jax.sharding import PartitionSpec as P

MESH = pl.DeviceIdType.MESH
JB_DEV = 60
ROWS = 8
AHEAD = 4
LAG = 4
PARTNERS = 15


def kernel(x_hbm, tile_col, keep, out_row, out_col, out, held, right_z, metas, mine, keep_z,
           meta_s, keep_s, weight_l, weight_r, part, part_z, outbox, inbox,
           local_sem, meta_send, meta_recv, y_send, y_recv, f_send, f_recv, z_send, z_recv,
           c_send, c_recv, p_send, p_recv, r_send, r_recv):
    i = lax.axis_index("inner")
    c = lax.axis_index("cols")
    y, z, core = c // 4, (c // 2) % 2, c % 2

    def ring(d, f):
        return (i, ((y + d) % 4) * 4 + z * 2 + (core + f) % 2)

    def inner(e):
        return ((i + e) % 8, c)

    across = (i, y * 4 + (1 - z) * 2 + core)

    def remote(src, dst, send, recv, to):
        return pltpu.make_async_remote_copy(
            src_ref=src, dst_ref=dst, send_sem=send, recv_sem=recv, device_id=to, device_id_type=MESH)

    load_x = pltpu.make_async_copy(x_hbm, held.at[0, pl.ds(0, ROWS)], local_sem.at[0])
    load_x.start()

    lane = lax.broadcasted_iota(jnp.int32, (8, 128), 1)
    mine[...] = jnp.where(lane == 0, out_row[0], jnp.where(lane == 1, out_col[0], 0))
    mine[0:4, 0:8] = tile_col[...]
    metas[0] = mine[...]
    metas[8 + i] = mine[...]
    part[...] = jnp.zeros_like(part)
    part_z[...] = jnp.zeros_like(part_z)

    others = [(d, f) for f in range(2) for d in range(4) if d + f > 0]
    barrier = pltpu.get_barrier_semaphore()
    for d, f in others:
        pl.semaphore_signal(barrier, inc=1, device_id=ring(d, f), device_id_type=MESH)
    for e in range(1, 8):
        pl.semaphore_signal(barrier, inc=1, device_id=inner(e), device_id_type=MESH)
    pl.semaphore_signal(barrier, inc=1, device_id=across, device_id_type=MESH)
    pl.semaphore_wait(barrier, PARTNERS)

    def send_meta():
        copies = []
        for d, f in others:
            n = f * 4 + (4 - d) % 4
            copies.append(remote(mine, metas.at[n], meta_send.at[n], meta_recv.at[n], ring(d, f)))
        for e in range(1, 8):
            copies.append(remote(mine, metas.at[8 + i], meta_send.at[7 + e], meta_recv.at[7 + e], inner(e)))
        copies.append(remote(keep, keep_z, meta_send.at[15], meta_recv.at[15], across))
        return copies

    def own_up(k):
        return remote(held.at[0, k], held.at[0, 24 + k], y_send.at[0, k], y_recv.at[0, k], ring(1, 0))

    def own_down(k):
        return remote(held.at[0, k], held.at[0, 8 + k], y_send.at[1, k], y_recv.at[1, k], ring(3, 0))

    def pass_up(k):
        return remote(held.at[0, 24 + k, pl.ds(0, 2)], held.at[0, 16 + k, pl.ds(0, 2)],
                      f_send.at[0, k], f_recv.at[0, k], ring(1, 0))

    def pass_down(k):
        return remote(held.at[0, 8 + k, pl.ds(2, 2)], held.at[0, 16 + k, pl.ds(2, 2)],
                      f_send.at[1, k], f_recv.at[1, k], ring(3, 0))

    def to_z(k):
        return remote(held.at[0, k], right_z.at[k], z_send.at[k], z_recv.at[k], across)

    def to_core(n):
        return remote(held.at[0, n], held.at[1, n], c_send.at[n], c_recv.at[n], ring(0, 1))

    own_to_core = remote(held.at[0, pl.ds(0, ROWS)], held.at[1, pl.ds(0, ROWS)],
                         c_send.at[0], c_recv.at[0], ring(0, 1))

    def to_reader(a):
        return remote(part_z.at[a], part.at[8 + a], p_send.at[a], p_recv.at[a], across)

    meta = send_meta()
    for copy in meta:
        copy.start()
    load_x.wait()
    for k in range(AHEAD):
        own_up(k).start()
        own_down(k).start()
        to_z(k).start()
    own_to_core.start()

    for copy in meta[7:14]:
        copy.wait_recv()
    meta_z = remote(metas.at[pl.ds(8, 8)], metas.at[pl.ds(16, 8)], meta_send.at[0], meta_recv.at[0], across)
    meta_z.start()
    for copy in meta[:7]:
        copy.wait_recv()
    meta[14].wait_recv()
    meta_z.wait_recv()
    stage = [
        pltpu.make_async_copy(metas, meta_s, local_sem.at[1]),
        pltpu.make_async_copy(keep, keep_s.at[0], local_sem.at[2]),
        pltpu.make_async_copy(keep_z, keep_s.at[1], local_sem.at[3]),
    ]
    for copy in stage:
        copy.start()
    for copy in stage:
        copy.wait()

    def weigh(n, carry):
        h, a = n // 8, n % 8
        holder = ((y + a % 4) % 4) * 4 + z * 2 + (core + a // 4) % 2
        row, col = jnp.int32(-1), jnp.int32(-1)
        for s in range(8):
            r = meta_s[8 + h * 8 + s, 4, 0]
            hit = (r >= holder * JB_DEV) & (r < holder * JB_DEV + JB_DEV)
            row = jnp.where(hit, r, row)
            col = jnp.where(hit, meta_s[8 + h * 8 + s, 4, 1], col)
        reader = h * (16 + i)
        for k in range(ROWS):
            at = (n * ROWS + k) * 4
            left = [(meta_s[a, p, k] == row).astype(jnp.int32) for p in range(4)]
            for p in range(4):
                weight_l[at + p] = left[p].astype(jnp.float32)
            for q in range(4):
                kept = sum(left[p] * keep_s[h, k, q, holder * 4 + p] for p in range(4))
                right = (meta_s[reader, q, k] == col).astype(jnp.int32)
                weight_r[at + q] = (right * kept).astype(jnp.float32)
        return carry

    lax.fori_loop(0, 16, weigh, 0)

    def halves(v):
        top = v.astype(jnp.bfloat16)
        return top, (v - top.astype(jnp.float32)).astype(jnp.bfloat16)

    def add(f, d, k):
        a = f * 4 + d
        for h in range(2):
            at = ((h * 8 + a) * ROWS + k) * 4
            left = sum(weight_l[at + p] * held[f, d * 8 + k, p] for p in range(4))
            if h == 0:
                right = sum(weight_r[at + q] * held[0, k, q] for q in range(4))
            else:
                right = sum(weight_r[at + q] * right_z[k, q] for q in range(4))
            lt, ll = halves(left.T)
            rt, rl = halves(right)
            product = (jnp.dot(lt, rt, preferred_element_type=jnp.float32)
                       + jnp.dot(lt, rl, preferred_element_type=jnp.float32)
                       + jnp.dot(ll, rt, preferred_element_type=jnp.float32))
            if h == 0:
                part[a] += product
            else:
                part_z[a] += product

    own_to_core.wait_recv()

    def step(t, carry):
        @pl.when(t < ROWS)
        def _():
            own_up(t).wait_recv()
            pass_up(t).start()
            to_core(24 + t).start()
            own_down(t).wait_recv()
            pass_down(t).start()
            to_core(8 + t).start()

            @pl.when(t + AHEAD < ROWS)
            def _():
                own_up(t + AHEAD).start()
                own_down(t + AHEAD).start()
                to_z(t + AHEAD).start()

            to_z(t).wait_recv()
            for f, d in ((0, 0), (1, 0), (0, 1), (0, 3)):
                add(f, d, t)

        @pl.when((t >= LAG) & (t < ROWS + LAG))
        def _():
            k = t - LAG
            pass_up(k).wait_recv()
            pass_down(k).wait_recv()
            to_core(16 + k).start()
            add(0, 2, k)

        @pl.when((t >= 1) & (t < ROWS + 1))
        def _():
            k = t - 1
            to_core(24 + k).wait_recv()
            add(1, 3, k)
            to_core(8 + k).wait_recv()
            add(1, 1, k)

        @pl.when(t == ROWS)
        def _():
            for a in (0, 1, 3, 4, 5, 7):
                to_reader(a).start()

        @pl.when(t >= LAG + 1)
        def _():
            k = t - LAG - 1
            to_core(16 + k).wait_recv()
            add(1, 2, k)

        return carry

    lax.fori_loop(0, ROWS + LAG + 1, step, 0)
    for a in (2, 6):
        to_reader(a).start()
    for a in range(8):
        to_reader(a).wait_recv()

    def place(s):
        slice_of = meta_s[8 + s, 4, 0] // JB_DEV
        far = jnp.where((slice_of // 2) % 2 == z, 0, 8)
        other = jnp.where(slice_of % 2 == core, 0, 4)
        return far + other + (slice_of // 4 - y + 4) % 4

    reduce = []
    for e in range(1, 8):
        outbox[e - 1] = part[place((i + e) % 8)]
        copy = remote(outbox.at[e - 1], inbox.at[e - 1], r_send.at[e - 1], r_recv.at[e - 1], inner(e))
        copy.start()
        reduce.append(copy)
    total = part[place(i)]
    for copy in reduce:
        copy.wait_recv()
    for e in range(7):
        total = total + inbox[e]
    out[0] = total

    for copy in meta:
        copy.wait_send()
    meta_z.wait_send()
    own_to_core.wait_send()

    def drain(k, carry):
        own_up(k).wait_send()
        own_down(k).wait_send()
        pass_up(k).wait_send()
        pass_down(k).wait_send()
        to_z(k).wait_send()
        to_core(8 + k).wait_send()
        to_core(16 + k).wait_send()
        to_core(24 + k).wait_send()
        to_reader(k).wait_send()
        return carry

    lax.fori_loop(0, ROWS, drain, 0)
    for copy in reduce:
        copy.wait_send()


def per_device(x_tiles, tile_col, keep_mask, out_rows, out_cols):
    vmem, smem = pltpu.VMEM, pltpu.SMEM
    dma = pltpu.SemaphoreType.DMA
    f32, i32 = jnp.float32, jnp.int32
    return pl.pallas_call(
        kernel,
        out_shape=jax.ShapeDtypeStruct((1, 128, 128), f32),
        in_specs=[
            pl.BlockSpec(memory_space=pl.ANY),
            pl.BlockSpec(memory_space=vmem),
            pl.BlockSpec(memory_space=vmem),
            pl.BlockSpec(memory_space=smem),
            pl.BlockSpec(memory_space=smem),
        ],
        out_specs=pl.BlockSpec(memory_space=vmem),
        scratch_shapes=[
            vmem((2, 32, 4, 128, 128), f32),
            vmem((8, 4, 128, 128), f32),
            vmem((24, 8, 128), i32),
            vmem((8, 128), i32),
            vmem((8, 4, 64), i32),
            smem((24, 8, 128), i32),
            smem((2, 8, 4, 64), i32),
            smem((512,), f32),
            smem((512,), f32),
            vmem((16, 128, 128), f32),
            vmem((8, 128, 128), f32),
            vmem((7, 128, 128), f32),
            vmem((7, 128, 128), f32),
            dma((4,)), dma((16,)), dma((16,)),
            dma((2, 8)), dma((2, 8)), dma((2, 8)), dma((2, 8)),
            dma((8,)), dma((8,)), dma((32,)), dma((32,)),
            dma((8,)), dma((8,)), dma((7,)), dma((7,)),
        ],
        compiler_params=pltpu.CompilerParams(
            collective_id=0, has_side_effects=True, vmem_limit_bytes=40 << 20),
        cost_estimate=pl.CostEstimate(flops=128 * 3 * 2 * 128**3, bytes_accessed=1 << 22, transcendentals=0),
        name="ring_product",
    )(x_tiles, tile_col.T, keep_mask.transpose(0, 2, 1), out_rows, out_cols)


def solution(mesh):
    return jax.shard_map(
        per_device,
        mesh=mesh,
        in_specs=(
            P("inner", "cols", None, None),
            P("inner", "cols"),
            P("inner", None, "cols"),
            P(("inner", "cols")),
            P(("inner", "cols")),
        ),
        out_specs=P(("inner", "cols"), None, None),
        check_vma=False,
    )
```

```python
import jax
import jax.numpy as jnp
from jax import lax
from jax.experimental import pallas as pl
from jax.experimental.pallas import tpu as pltpu
from jax.sharding import PartitionSpec as P

MESH = pl.DeviceIdType.MESH
JB_DEV = 60
ROWS = 8
AHEAD = 4
LAG = 4
PARTNERS = 15


def kernel(x_hbm, tile_col_hbm, keep, out_row, out_col, out, held, right_z, metas, mine, tile_col, keep_z,
           meta_s, keep_s, weight_l, weight_r, part, part_z, outbox, inbox,
           local_sem, meta_send, meta_recv, y_send, y_recv, f_send, f_recv, z_send, z_recv,
           c_send, c_recv, p_send, p_recv, r_send, r_recv):
    i = lax.axis_index("inner")
    c = lax.axis_index("cols")
    y, z, core = c // 4, (c // 2) % 2, c % 2

    def ring(d, f):
        return (i, ((y + d) % 4) * 4 + z * 2 + (core + f) % 2)

    def inner(e):
        return ((i + e) % 8, c)

    across = (i, y * 4 + (1 - z) * 2 + core)

    def remote(src, dst, send, recv, to):
        return pltpu.make_async_remote_copy(
            src_ref=src, dst_ref=dst, send_sem=send, recv_sem=recv, device_id=to, device_id_type=MESH)

    load_x = pltpu.make_async_copy(x_hbm, held.at[0, pl.ds(0, ROWS)], local_sem.at[0])
    load_x.start()
    load_col = pltpu.make_async_copy(tile_col_hbm, tile_col, local_sem.at[1])
    load_col.start()
    load_keep = pltpu.make_async_copy(keep, keep_s.at[0], local_sem.at[2])
    load_keep.start()

    others = [(d, f) for f in range(2) for d in range(4) if d + f > 0]
    barrier = pltpu.get_barrier_semaphore()
    for d, f in others:
        pl.semaphore_signal(barrier, inc=1, device_id=ring(d, f), device_id_type=MESH)
    for e in range(1, 8):
        pl.semaphore_signal(barrier, inc=1, device_id=inner(e), device_id_type=MESH)
    pl.semaphore_signal(barrier, inc=1, device_id=across, device_id_type=MESH)

    load_col.wait()
    lane = lax.broadcasted_iota(jnp.int32, (8, 128), 1)
    mine[...] = jnp.where(lane == 0, out_row[0], jnp.where(lane == 1, out_col[0], 0))
    mine[0:4, 0:8] = tile_col[...]
    metas[0] = mine[...]
    metas[8 + i] = mine[...]
    part[...] = jnp.zeros_like(part)
    part_z[...] = jnp.zeros_like(part_z)
    pl.semaphore_wait(barrier, PARTNERS)

    def send_meta():
        copies = []
        for d, f in others:
            n = f * 4 + (4 - d) % 4
            copies.append(remote(mine, metas.at[n], meta_send.at[n], meta_recv.at[n], ring(d, f)))
        for e in range(1, 8):
            copies.append(remote(mine, metas.at[8 + i], meta_send.at[7 + e], meta_recv.at[7 + e], inner(e)))
        copies.append(remote(keep, keep_z, meta_send.at[15], meta_recv.at[15], across))
        return copies

    def own_up(k):
        return remote(held.at[0, k], held.at[0, 24 + k], y_send.at[0, k], y_recv.at[0, k], ring(1, 0))

    def own_down(k):
        return remote(held.at[0, k], held.at[0, 8 + k], y_send.at[1, k], y_recv.at[1, k], ring(3, 0))

    def pass_up(k):
        return remote(held.at[0, 24 + k, pl.ds(0, 2)], held.at[0, 16 + k, pl.ds(0, 2)],
                      f_send.at[0, k], f_recv.at[0, k], ring(1, 0))

    def pass_down(k):
        return remote(held.at[0, 8 + k, pl.ds(2, 2)], held.at[0, 16 + k, pl.ds(2, 2)],
                      f_send.at[1, k], f_recv.at[1, k], ring(3, 0))

    def to_z(k):
        return remote(held.at[0, k], right_z.at[k], z_send.at[k], z_recv.at[k], across)

    def to_core(n):
        return remote(held.at[0, n], held.at[1, n], c_send.at[n], c_recv.at[n], ring(0, 1))

    own_to_core = remote(held.at[0, pl.ds(0, ROWS)], held.at[1, pl.ds(0, ROWS)],
                         c_send.at[0], c_recv.at[0], ring(0, 1))

    def to_reader(a):
        return remote(part_z.at[a], part.at[8 + a], p_send.at[a], p_recv.at[a], across)

    meta = send_meta()
    for copy in meta:
        copy.start()
    load_x.wait()
    for k in range(AHEAD):
        own_up(k).start()
        own_down(k).start()
    own_to_core.start()

    for copy in meta[7:14]:
        copy.wait_recv()
    meta_z = remote(metas.at[pl.ds(8, 8)], metas.at[pl.ds(16, 8)], meta_send.at[0], meta_recv.at[0], across)
    meta_z.start()
    for k in range(AHEAD):
        to_z(k).start()
    for copy in meta[:7]:
        copy.wait_recv()
    meta[14].wait_recv()
    meta_z.wait_recv()
    stage = [
        pltpu.make_async_copy(metas, meta_s, local_sem.at[1]),
        pltpu.make_async_copy(keep_z, keep_s.at[1], local_sem.at[3]),
    ]
    for copy in stage:
        copy.start()
    for copy in stage:
        copy.wait()
    load_keep.wait()

    def weigh(n, carry):
        h, a = n // 8, n % 8
        holder = ((y + a % 4) % 4) * 4 + z * 2 + (core + a // 4) % 2
        row, col = jnp.int32(-1), jnp.int32(-1)
        for s in range(8):
            r = meta_s[8 + h * 8 + s, 4, 0]
            hit = (r >= holder * JB_DEV) & (r < holder * JB_DEV + JB_DEV)
            row = jnp.where(hit, r, row)
            col = jnp.where(hit, meta_s[8 + h * 8 + s, 4, 1], col)
        reader = h * (16 + i)
        for k in range(ROWS):
            at = (n * ROWS + k) * 4
            left = [(meta_s[a, p, k] == row).astype(jnp.int32) for p in range(4)]
            for p in range(4):
                weight_l[at + p] = left[p].astype(jnp.float32)
            for q in range(4):
                kept = sum(left[p] * keep_s[h, k, q, holder * 4 + p] for p in range(4))
                right = (meta_s[reader, q, k] == col).astype(jnp.int32)
                weight_r[at + q] = (right * kept).astype(jnp.float32)
        return carry

    lax.fori_loop(0, 16, weigh, 0)

    def halves(v):
        top = v.astype(jnp.bfloat16)
        return top, (v - top.astype(jnp.float32)).astype(jnp.bfloat16)

    def add(f, d, k):
        a = f * 4 + d
        for h in range(2):
            at = ((h * 8 + a) * ROWS + k) * 4
            left = sum(weight_l[at + p] * held[f, d * 8 + k, p] for p in range(4))
            if h == 0:
                right = sum(weight_r[at + q] * held[0, k, q] for q in range(4))
            else:
                right = sum(weight_r[at + q] * right_z[k, q] for q in range(4))
            lt, ll = halves(left.T)
            rt, rl = halves(right)
            product = (jnp.dot(lt, rt, preferred_element_type=jnp.float32)
                       + jnp.dot(lt, rl, preferred_element_type=jnp.float32)
                       + jnp.dot(ll, rt, preferred_element_type=jnp.float32))
            if h == 0:
                part[a] += product
            else:
                part_z[a] += product

    own_to_core.wait_recv()

    def step(t, carry):
        @pl.when(t < ROWS)
        def _():
            own_up(t).wait_recv()
            pass_up(t).start()
            to_core(24 + t).start()
            own_down(t).wait_recv()
            pass_down(t).start()
            to_core(8 + t).start()

            @pl.when(t + AHEAD < ROWS)
            def _():
                own_up(t + AHEAD).start()
                own_down(t + AHEAD).start()
                to_z(t + AHEAD).start()

            to_z(t).wait_recv()
            for f, d in ((0, 0), (1, 0), (0, 1), (0, 3)):
                add(f, d, t)

        @pl.when((t >= LAG) & (t < ROWS + LAG))
        def _():
            k = t - LAG
            pass_up(k).wait_recv()
            pass_down(k).wait_recv()
            to_core(16 + k).start()
            add(0, 2, k)

        @pl.when((t >= 1) & (t < ROWS + 1))
        def _():
            k = t - 1
            to_core(24 + k).wait_recv()
            add(1, 3, k)
            to_core(8 + k).wait_recv()
            add(1, 1, k)

        @pl.when(t == ROWS)
        def _():
            for a in (0, 1, 3, 4, 5, 7):
                to_reader(a).start()

        @pl.when(t >= LAG + 1)
        def _():
            k = t - LAG - 1
            to_core(16 + k).wait_recv()
            add(1, 2, k)

        return carry

    lax.fori_loop(0, ROWS + LAG + 1, step, 0)
    for a in (2, 6):
        to_reader(a).start()
    for a in range(8):
        to_reader(a).wait_recv()

    def place(s):
        slice_of = meta_s[8 + s, 4, 0] // JB_DEV
        far = jnp.where((slice_of // 2) % 2 == z, 0, 8)
        other = jnp.where(slice_of % 2 == core, 0, 4)
        return far + other + (slice_of // 4 - y + 4) % 4

    reduce = []
    for e in range(1, 8):
        outbox[e - 1] = part[place((i + e) % 8)]
        copy = remote(outbox.at[e - 1], inbox.at[e - 1], r_send.at[e - 1], r_recv.at[e - 1], inner(e))
        copy.start()
        reduce.append(copy)
    total = part[place(i)]
    for copy in reduce:
        copy.wait_recv()
    for e in range(7):
        total = total + inbox[e]
    out[0] = total

    for copy in meta:
        copy.wait_send()
    meta_z.wait_send()
    own_to_core.wait_send()

    def drain(k, carry):
        own_up(k).wait_send()
        own_down(k).wait_send()
        pass_up(k).wait_send()
        pass_down(k).wait_send()
        to_z(k).wait_send()
        to_core(8 + k).wait_send()
        to_core(16 + k).wait_send()
        to_core(24 + k).wait_send()
        to_reader(k).wait_send()
        return carry

    lax.fori_loop(0, ROWS, drain, 0)
    for copy in reduce:
        copy.wait_send()


def per_device(x_tiles, tile_col, keep_mask, out_rows, out_cols):
    vmem, smem = pltpu.VMEM, pltpu.SMEM
    dma = pltpu.SemaphoreType.DMA
    f32, i32 = jnp.float32, jnp.int32
    return pl.pallas_call(
        kernel,
        out_shape=jax.ShapeDtypeStruct((1, 128, 128), f32),
        in_specs=[
            pl.BlockSpec(memory_space=pltpu.HBM),
            pl.BlockSpec(memory_space=pltpu.HBM),
            pl.BlockSpec(memory_space=pltpu.HBM),
            pl.BlockSpec(memory_space=smem),
            pl.BlockSpec(memory_space=smem),
        ],
        out_specs=pl.BlockSpec(memory_space=vmem),
        scratch_shapes=[
            vmem((2, 32, 4, 128, 128), f32),
            vmem((8, 4, 128, 128), f32),
            vmem((24, 8, 128), i32),
            vmem((8, 128), i32),
            vmem((4, 8), i32),
            vmem((8, 4, 64), i32),
            smem((24, 8, 128), i32),
            smem((2, 8, 4, 64), i32),
            smem((512,), f32),
            smem((512,), f32),
            vmem((16, 128, 128), f32),
            vmem((8, 128, 128), f32),
            vmem((7, 128, 128), f32),
            vmem((7, 128, 128), f32),
            dma((4,)), dma((16,)), dma((16,)),
            dma((2, 8)), dma((2, 8)), dma((2, 8)), dma((2, 8)),
            dma((8,)), dma((8,)), dma((32,)), dma((32,)),
            dma((8,)), dma((8,)), dma((7,)), dma((7,)),
        ],
        compiler_params=pltpu.CompilerParams(
            collective_id=0, has_side_effects=True, vmem_limit_bytes=59 << 20),
        cost_estimate=pl.CostEstimate(flops=128 * 3 * 2 * 128**3, bytes_accessed=1 << 22, transcendentals=0),
        name="ring_product",
    )(x_tiles, tile_col.T, keep_mask.transpose(0, 2, 1), out_rows, out_cols)


def solution(mesh):
    return jax.shard_map(
        per_device,
        mesh=mesh,
        in_specs=(
            P("inner", "cols", None, None),
            P("inner", "cols"),
            P("inner", None, "cols"),
            P(("inner", "cols")),
            P(("inner", "cols")),
        ),
        out_specs=P(("inner", "cols"), None, None),
        check_vma=False,
    )
```

```python
import jax
import jax.numpy as jnp
from jax import lax
from jax.experimental import pallas as pl
from jax.experimental.pallas import tpu as pltpu
from jax.sharding import PartitionSpec as P

MESH = pl.DeviceIdType.MESH
JB_DEV = 60
ROWS = 8
AHEAD = 8
LAG = 8
PARTNERS = 17


def kernel(x_hbm, tile_col_hbm, keep, out_row, out_col, out, held, right_z, passed, picked, metas, mine, tile_col,
           keeps, meta_s, keep_s, weight_l, weight_r, part, part_z, between, outbox, inbox,
           local_sem, meta_send, meta_recv, list_send, list_recv, y_send, y_recv, f_send, f_recv, z_send, z_recv,
           c_send, c_recv, p_send, p_recv, b_send, b_recv, r_send, r_recv):
    i = lax.axis_index("inner")
    c = lax.axis_index("cols")
    y, z, core = c // 4, (c // 2) % 2, c % 2

    def ring(d, f):
        return (i, ((y + d) % 4) * 4 + z * 2 + (core + f) % 2)

    def inner(e):
        return ((i + e) % 8, c)

    def over_y(d, on):
        return (i, ((y + d) % 4) * 4 + z * 2 + on)

    def over(d, on):
        return (i, ((y + d) % 4) * 4 + (1 - z) * 2 + on)

    across = over(0, core)

    def remote(src, dst, send, recv, to):
        return pltpu.make_async_remote_copy(
            src_ref=src, dst_ref=dst, send_sem=send, recv_sem=recv, device_id=to, device_id_type=MESH)

    load_x = pltpu.make_async_copy(x_hbm, held.at[0, pl.ds(0, ROWS)], local_sem.at[0])
    load_x.start()
    load_col = pltpu.make_async_copy(tile_col_hbm, tile_col, local_sem.at[1])
    load_col.start()
    load_keep = pltpu.make_async_copy(keep, keeps.at[0], local_sem.at[2])
    load_keep.start()

    others = [(d, f) for f in range(2) for d in range(4) if d + f > 0]
    barrier = pltpu.get_barrier_semaphore()
    for d, f in others:
        pl.semaphore_signal(barrier, inc=1, device_id=ring(d, f), device_id_type=MESH)
    for e in range(1, 8):
        pl.semaphore_signal(barrier, inc=1, device_id=inner(e), device_id_type=MESH)
    for to in (across, over(1, 0), over(3, 1)):
        pl.semaphore_signal(barrier, inc=1, device_id=to, device_id_type=MESH)

    load_col.wait()
    lane = lax.broadcasted_iota(jnp.int32, (8, 128), 1)
    mine[...] = jnp.where(lane == 0, out_row[0], jnp.where(lane == 1, out_col[0], 0))
    mine[0:4, 0:8] = tile_col[...]
    metas[0] = mine[...]
    metas[8 + i] = mine[...]
    part[...] = jnp.zeros_like(part)
    part_z[...] = jnp.zeros_like(part_z)
    between[...] = jnp.zeros_like(between)
    pl.semaphore_wait(barrier, PARTNERS)

    slots = [remote(mine, metas.at[8 + i], meta_send.at[7 + e], meta_recv.at[7 + e], inner(e)) for e in range(1, 8)]
    holders = []
    for d, f in others:
        n = f * 4 + (4 - d) % 4
        holders.append(remote(mine, metas.at[n], meta_send.at[n], meta_recv.at[n], ring(d, f)))

    def lists(h, to):
        return remote(metas.at[pl.ds(8, 8)], metas.at[pl.ds(8 + 8 * h, 8)], list_send.at[h], list_recv.at[h], to)

    def filters(h, to):
        return remote(keep, keeps.at[h], list_send.at[5 + h], list_recv.at[5 + h], to)

    filter_copies = [filters(1, across), filters(2, ring(3, 0)), filters(3, ring(1, 0))]
    list_copies = [lists(1, across), lists(2, ring(3, 0)), lists(3, ring(1, 0))]

    def diagonal(on):
        h = 4 + core
        return remote(metas.at[pl.ds(8, 8)], metas.at[pl.ds(8 + 8 * h, 8)], list_send.at[9 + on], list_recv.at[h],
                      over(3 + 2 * core, on))

    diagonal_copies = [diagonal(0), diagonal(1)]

    def own_up(k):
        return remote(held.at[0, k], held.at[0, 24 + k], y_send.at[0, k], y_recv.at[0, k], ring(1, 0))

    def own_down(k):
        return remote(held.at[0, k], held.at[0, 8 + k], y_send.at[1, k], y_recv.at[1, k], ring(3, 0))

    def pass_up(k):
        return remote(picked.at[0, k], passed.at[core, k], f_send.at[0, k], f_recv.at[core, k], over_y(1, 0))

    def pass_down(k):
        return remote(picked.at[1, k], passed.at[1 - core, k], f_send.at[1, k], f_recv.at[1 - core, k], over_y(3, 1))

    def arrived(f, k):
        return remote(picked.at[f, k], passed.at[f, k], f_send.at[f, k], f_recv.at[f, k], over_y(1, 0))

    def to_z(k):
        return remote(held.at[0, k], right_z.at[k], z_send.at[k], z_recv.at[k], across)

    def to_core(n):
        return remote(held.at[0, n], held.at[1, n], c_send.at[n], c_recv.at[n], ring(0, 1))

    own_to_core = remote(held.at[0, pl.ds(0, ROWS)], held.at[1, pl.ds(0, ROWS)],
                         c_send.at[0], c_recv.at[0], ring(0, 1))

    def to_reader(a):
        return remote(part_z.at[a], part.at[8 + a], p_send.at[a], p_recv.at[a], across)

    back_up = remote(between.at[0], part.at[2], b_send.at[0], b_recv.at[0], ring(1, 0))
    back_down = remote(between.at[1], part.at[6], b_send.at[1], b_recv.at[1], ring(3, 0))

    def start_rows(k):
        own_up(k).start()
        own_down(k).start()
        to_z(k).start()

    for copy in slots:
        copy.start()
    load_x.wait()
    start_rows(0)
    for copy in holders + filter_copies:
        copy.start()
    for copy in slots:
        copy.wait_recv()
    for copy in list_copies + diagonal_copies:
        copy.start()
    for k in range(1, AHEAD):
        start_rows(k)
    own_to_core.start()
    for copy in holders + filter_copies + list_copies:
        copy.wait_recv()
    for h in (4, 5):
        remote(metas.at[pl.ds(8, 8)], metas.at[pl.ds(8 + 8 * h, 8)], list_send.at[5 + h], list_recv.at[h], across).wait_recv()
    load_keep.wait()
    stage = [
        pltpu.make_async_copy(metas, meta_s, local_sem.at[1]),
        pltpu.make_async_copy(keeps, keep_s, local_sem.at[3]),
    ]
    for copy in stage:
        copy.start()
    for copy in stage:
        copy.wait()

    def weigh(n, carry):
        h = jnp.where(n < 16, n // 8, n - 14)
        a = jnp.where(n < 16, n % 8, jnp.where(n == 17, 5, jnp.where(n == 19, 1, 3)))
        holder = ((y + a % 4) % 4) * 4 + z * 2 + (core + a // 4) % 2
        row, col = jnp.int32(-1), jnp.int32(-1)
        for s in range(8):
            r = meta_s[8 + h * 8 + s, 4, 0]
            hit = (r >= holder * JB_DEV) & (r < holder * JB_DEV + JB_DEV)
            row = jnp.where(hit, r, row)
            col = jnp.where(hit, meta_s[8 + h * 8 + s, 4, 1], col)
        reader = 8 + h * 8 + i
        filter_of = jnp.minimum(h, 3)
        for k in range(ROWS):
            at = (n * ROWS + k) * 4
            left = [(meta_s[a, p, k] == row).astype(jnp.int32) for p in range(4)]
            for p in range(4):
                weight_l[at + p] = left[p].astype(jnp.float32)
            for q in range(4):
                kept = sum(left[p] * keep_s[filter_of, k, q, holder * 4 + p] for p in range(4))
                right = (meta_s[reader, q, k] == col).astype(jnp.int32)
                weight_r[at + q] = (right * kept).astype(jnp.float32)
        return carry

    lax.fori_loop(0, 20, weigh, 0)

    def halves(v):
        top = v.astype(jnp.bfloat16)
        return top, (v - top.astype(jnp.float32)).astype(jnp.bfloat16)

    def choose(weights, n, k, row):
        at = (n * ROWS + k) * 4
        return sum(weights[at + p] * row[p] for p in range(4))

    def multiply(left, right):
        lt, ll = halves(left.T)
        rt, rl = halves(right)
        return (jnp.dot(lt, rt, preferred_element_type=jnp.float32)
                + jnp.dot(lt, rl, preferred_element_type=jnp.float32)
                + jnp.dot(ll, rt, preferred_element_type=jnp.float32))

    def add(f, d, k):
        a = f * 4 + d
        row = held.at[f, d * 8 + k]
        part[a] += multiply(choose(weight_l, a, k, row), choose(weight_r, a, k, held.at[0, k]))
        part_z[a] += multiply(choose(weight_l, 8 + a, k, row), choose(weight_r, 8 + a, k, right_z.at[k]))

    def add_passed(f, k):
        a = f * 4 + 2
        part_z[a] += multiply(passed[f, k], choose(weight_r, 8 + a, k, right_z.at[k]))

    def add_between(g, k):
        left = held.at[0, 24 + k] if g == 0 else held.at[1, 8 + k]
        right = held.at[0, 8 + k] if g == 0 else held.at[0, 24 + k]
        between[g] += multiply(choose(weight_l, 16 + g, k, left), choose(weight_r, 16 + g, k, right))

    own_to_core.wait_recv()

    def step(t, carry):
        @pl.when(t < ROWS)
        def _():
            own_up(t).wait_recv()
            picked[0, t] = choose(weight_l, 18, t, held.at[0, 24 + t])
            pass_up(t).start()
            to_core(24 + t).start()
            own_down(t).wait_recv()
            picked[1, t] = choose(weight_l, 19, t, held.at[0, 8 + t])
            pass_down(t).start()
            to_core(8 + t).start()

            @pl.when(t + AHEAD < ROWS)
            def _():
                start_rows(t + AHEAD)

            to_z(t).wait_recv()
            for f, d in ((0, 0), (1, 0), (0, 1), (0, 3)):
                add(f, d, t)
            add_between(0, t)

        @pl.when((t >= 1) & (t < ROWS + 1))
        def _():
            k = t - 1
            to_core(8 + k).wait_recv()
            add(1, 1, k)
            add_between(1, k)
            to_core(24 + k).wait_recv()
            add(1, 3, k)

        @pl.when(t == ROWS)
        def _():
            for a in (0, 1, 3, 4, 5, 7):
                to_reader(a).start()
            back_up.start()
            back_down.start()

        @pl.when(t >= LAG)
        def _():
            k = t - LAG
            for f in range(2):
                arrived(f, k).wait_recv()
                add_passed(f, k)

        return carry

    lax.fori_loop(0, ROWS + LAG, step, 0)
    for a in (2, 6):
        to_reader(a).start()
    for a in range(8):
        to_reader(a).wait_recv()
    back_up.wait_recv()
    back_down.wait_recv()

    def place(s):
        slice_of = meta_s[8 + s, 4, 0] // JB_DEV
        far = jnp.where((slice_of // 2) % 2 == z, 0, 8)
        other = jnp.where(slice_of % 2 == core, 0, 4)
        return far + other + (slice_of // 4 - y + 4) % 4

    reduce = []
    for e in range(1, 8):
        outbox[e - 1] = part[place((i + e) % 8)]
        copy = remote(outbox.at[e - 1], inbox.at[e - 1], r_send.at[e - 1], r_recv.at[e - 1], inner(e))
        copy.start()
        reduce.append(copy)
    total = part[place(i)]
    for copy in reduce:
        copy.wait_recv()
    for e in range(7):
        total = total + inbox[e]
    out[0] = total

    for copy in slots + holders + filter_copies + list_copies + diagonal_copies + [own_to_core, back_up, back_down]:
        copy.wait_send()

    def drain(k, carry):
        own_up(k).wait_send()
        own_down(k).wait_send()
        pass_up(k).wait_send()
        pass_down(k).wait_send()
        to_z(k).wait_send()
        to_core(8 + k).wait_send()
        to_core(24 + k).wait_send()
        to_reader(k).wait_send()
        return carry

    lax.fori_loop(0, ROWS, drain, 0)
    for copy in reduce:
        copy.wait_send()


def per_device(x_tiles, tile_col, keep_mask, out_rows, out_cols):
    vmem, smem = pltpu.VMEM, pltpu.SMEM
    dma = pltpu.SemaphoreType.DMA
    f32, i32 = jnp.float32, jnp.int32
    return pl.pallas_call(
        kernel,
        out_shape=jax.ShapeDtypeStruct((1, 128, 128), f32),
        in_specs=[
            pl.BlockSpec(memory_space=pltpu.HBM),
            pl.BlockSpec(memory_space=pltpu.HBM),
            pl.BlockSpec(memory_space=pltpu.HBM),
            pl.BlockSpec(memory_space=smem),
            pl.BlockSpec(memory_space=smem),
        ],
        out_specs=pl.BlockSpec(memory_space=vmem),
        scratch_shapes=[
            vmem((2, 32, 4, 128, 128), f32),
            vmem((8, 4, 128, 128), f32),
            vmem((2, 8, 128, 128), f32),
            vmem((2, 8, 128, 128), f32),
            vmem((56, 8, 128), i32),
            vmem((8, 128), i32),
            vmem((4, 8), i32),
            vmem((4, 8, 4, 64), i32),
            smem((56, 8, 128), i32),
            smem((4, 8, 4, 64), i32),
            smem((640,), f32),
            smem((640,), f32),
            vmem((16, 128, 128), f32),
            vmem((8, 128, 128), f32),
            vmem((2, 128, 128), f32),
            vmem((7, 128, 128), f32),
            vmem((7, 128, 128), f32),
            dma((4,)), dma((16,)), dma((16,)), dma((11,)), dma((11,)),
            dma((2, 8)), dma((2, 8)), dma((2, 8)), dma((2, 8)),
            dma((8,)), dma((8,)), dma((32,)), dma((32,)),
            dma((8,)), dma((8,)), dma((2,)), dma((2,)), dma((7,)), dma((7,)),
        ],
        compiler_params=pltpu.CompilerParams(
            collective_id=0, has_side_effects=True, vmem_limit_bytes=59 << 20),
        cost_estimate=pl.CostEstimate(flops=128 * 3 * 2 * 128**3, bytes_accessed=1 << 22, transcendentals=0),
        name="ring_product",
    )(x_tiles, tile_col.T, keep_mask.transpose(0, 2, 1), out_rows, out_cols)


def solution(mesh):
    return jax.shard_map(
        per_device,
        mesh=mesh,
        in_specs=(
            P("inner", "cols", None, None),
            P("inner", "cols"),
            P("inner", None, "cols"),
            P(("inner", "cols")),
            P(("inner", "cols")),
        ),
        out_specs=P(("inner", "cols"), None, None),
        check_vma=False,
    )
```

```python
import jax
import jax.numpy as jnp
from jax import lax
from jax.experimental import pallas as pl
from jax.experimental.pallas import tpu as pltpu
from jax.sharding import PartitionSpec as P

MESH = pl.DeviceIdType.MESH
JB_DEV = 60
PARTNERS = 16
STEPS = ((2, 1), (1, 1), (3, 1), (2, 0), (1, 0), (3, 0), (0, 1))
PARTS = ((0, 48, (0, 1, 2)), (48, 40, (1, 2, 0)), (88, 40, (2, 0, 1)))


def kernel(x, tile_col_hbm, keep_hbm, out_row, out_col, out, held, products, tile_col, keep, mine, slots, notes, heard,
           heard_s, left_s, right_s, gate_s, one_a, one_b, one_c, two_a, two_b, two_c, three_a, three_b, three_c,
           sum_a, sum_b, sum_c, line_a, line_b, line_c,
           local_sem, s_send, s_recv, n_send, n_recv, g_send, g_recv, c_send, c_recv, h_send, h_recv, r_send, r_recv):
    i = lax.axis_index("inner")
    c = lax.axis_index("cols")
    core = c % 2
    at = (i // 2, c // 4, (i % 2) * 2 + (c // 2) % 2)
    z_hi, z_lo = i % 2, (c // 2) % 2
    home = at[1] * 2 + z_lo

    def device(place, on):
        px, py, pz = place
        return (px * 2 + pz // 2, py * 4 + (pz % 2) * 2 + on)

    def row_home(step):
        py, pz = (at[1] + step[0]) % 4, (z_lo + step[1]) % 2
        return py * 2 + pz, device((at[0], py, z_hi * 2 + pz), core)

    def inner(e):
        return ((i + e) % 8, c)

    def along(axis, d):
        return device(tuple((p + d) % 4 if n == axis else p for n, p in enumerate(at)), core)

    twin = device(at, 1 - core)

    def remote(src, dst, send, recv, to):
        return pltpu.make_async_remote_copy(
            src_ref=src, dst_ref=dst, send_sem=send, recv_sem=recv, device_id=to, device_id_type=MESH)

    load_col = pltpu.make_async_copy(tile_col_hbm, tile_col, local_sem.at[0])
    load_keep = pltpu.make_async_copy(keep_hbm, keep, local_sem.at[1])
    load_own = pltpu.make_async_copy(x.at[home], held.at[pl.ds(home * 4, 4)], local_sem.at[2])
    load_col.start()
    load_keep.start()
    load_own.start()

    barrier = pltpu.get_barrier_semaphore()
    partners = [row_home(step)[1] for step in STEPS] + [inner(e) for e in range(1, 8)]
    partners += [twin, device((at[0], at[1], 3 - at[2]), core)]
    for to in partners:
        pl.semaphore_signal(barrier, inc=1, device_id=to, device_id_type=MESH)

    sublane = lax.broadcasted_iota(jnp.int32, (8, 128), 0)
    lane = lax.broadcasted_iota(jnp.int32, (8, 128), 1)
    mine[...] = jnp.where(sublane == 4, out_row[0], jnp.where(sublane == 5, out_col[0], 0))
    slots[i] = mine[...]
    load_col.wait()
    load_keep.wait()
    pl.semaphore_wait(barrier, PARTNERS)

    slot_copies = [remote(mine, slots.at[i], s_send.at[e - 1], s_recv.at[e - 1], inner(e)) for e in range(1, 8)]
    for copy in slot_copies:
        copy.start()

    def send_blocks(p):
        for j, step in enumerate(STEPS):
            row, to = row_home(step)
            remote(x.at[row, p], held.at[home * 4 + p], g_send.at[j], g_recv.at[home], to).start()

    send_blocks(0)
    for copy in slot_copies:
        copy.wait_recv()

    listed = jnp.zeros((8, 128), jnp.int32)
    for s in range(8):
        listed = jnp.where(lane == s, slots[s], listed)
    for k in range(8):
        notes[k] = listed
        notes[k, 0:4, 0:64] = keep[k]
        notes[k, 0:4, 64:128] = jnp.broadcast_to(tile_col[:, k:k + 1], (4, 64))
    heard[home] = notes[home]

    def note(j):
        row, to = row_home(STEPS[j])
        return remote(notes.at[row], heard.at[home], n_send.at[j], n_recv.at[home], to)

    for j in range(7):
        note(j).start()
    for p in range(1, 4):
        send_blocks(p)

    def from_chip(step):
        source, to = row_home(step)
        return source, remote(notes.at[0], heard.at[source], n_send.at[0], n_recv.at[source], to), remote(
            held.at[pl.ds(0, 4)], held.at[pl.ds(source * 4, 4)], g_send.at[0], g_recv.at[source], to)

    for step in STEPS:
        from_chip(step)[1].wait_recv()
    share_notes = remote(heard.at[pl.ds(0, 8)], heard.at[pl.ds(8, 8)], h_send.at[0], h_recv.at[0], twin)
    share_notes.start()

    def share(source):
        return remote(held.at[pl.ds(source * 4, 4)], held.at[pl.ds(32 + source * 4, 4)],
                      c_send.at[source], c_recv.at[source], twin)

    load_own.wait()
    share(home).start()
    share_notes.wait_recv()
    stage = pltpu.make_async_copy(heard, heard_s, local_sem.at[3])
    stage.start()
    stage.wait()

    def find(n, carry):
        sx, sy, sz = n // 16, (n // 4) % 4, n % 4
        index, chip = sx * 2 + sz // 2, sy * 2 + sz % 2
        row, col = heard_s[chip, 4, index], heard_s[chip, 5, index]
        left_slice = row // JB_DEV
        holder = jnp.where(left_slice % 2 == core, 0, 8) + left_slice // 2
        p, q, stored_l, stored_r = jnp.int32(0), jnp.int32(0), jnp.int32(0), jnp.int32(0)
        for r in range(4):
            hit = heard_s[holder, r, 64] == row
            p, stored_l = jnp.where(hit, r, p), jnp.where(hit, 1, stored_l)
            hit = heard_s[chip, r, 64] == col
            q, stored_r = jnp.where(hit, r, q), jnp.where(hit, 1, stored_r)
        left_s[n] = holder * 4 + p
        right_s[n] = chip * 4 + q
        gate_s[n] = (heard_s[chip, q, left_slice * 4 + p] * stored_l * stored_r).astype(jnp.float32)
        return carry

    lax.fori_loop(0, 64, find, 0)

    for step in STEPS[::-1]:
        source, _, blocks = from_chip(step)
        blocks.wait_recv()
        share(source).start()
    for source in range(8):
        share(source).wait_recv()

    def halves(v):
        top = v.astype(jnp.bfloat16)
        return top, (v - top.astype(jnp.float32)).astype(jnp.bfloat16)

    def product(n):
        lt, ll = halves(held[left_s[n]].T)
        rt, rl = halves(held[right_s[n]] * gate_s[n])
        return (jnp.dot(lt, rt, preferred_element_type=jnp.float32)
                + jnp.dot(lt, rl, preferred_element_type=jnp.float32)
                + jnp.dot(ll, rt, preferred_element_type=jnp.float32))

    ones, twos, threes = (one_a, one_b, one_c), (two_a, two_b, two_c), (three_a, three_b, three_c)
    sums, lines = (sum_a, sum_b, sum_c), (line_a, line_b, line_c)

    def pick(axes_left, axis, where):
        return tuple(where if a == axis else slice(None) for a in axes_left)

    def first(part, d):
        start, rows, (axis, _, _) = PARTS[part]
        cut = pick((0, 1, 2), axis, (at[axis] + d) % 4) + (pl.ds(start, rows),)
        return remote(products.at[cut], ones[part].at[d - 1], r_send.at[part, d - 1], r_recv.at[part, d - 1], along(axis, d))

    def second(part, d):
        _, _, (gone, axis, _) = PARTS[part]
        cut = pick([a for a in range(3) if a != gone], axis, (at[axis] + d) % 4)
        return remote(sums[part].at[cut], twos[part].at[d - 1], r_send.at[part, 2 + d], r_recv.at[part, 2 + d], along(axis, d))

    def third(part, d):
        _, _, (_, _, axis) = PARTS[part]
        return remote(lines[part].at[(at[axis] + d) % 4], threes[part].at[d - 1],
                      r_send.at[part, 5 + d], r_recv.at[part, 5 + d], along(axis, d))

    def slab(px):
        def body(n, carry):
            products[px, n // 4, n % 4] = product(px * 16 + n)
            return carry

        lax.fori_loop(0, 16, body, 0)

    for d in (2, 1, 3):
        slab((at[0] + d) % 4)
        first(0, d).start()
    slab(at[0])
    for d in (2, 1, 3):
        for part in (1, 2):
            first(part, d).start()

    for part, (start, rows, (axis, _, _)) in enumerate(PARTS):
        for d in range(1, 4):
            first(part, d).wait_recv()
        cut = pick((0, 1, 2), axis, at[axis]) + (pl.ds(start, rows),)
        sums[part][...] = products[cut] + ones[part][0] + ones[part][1] + ones[part][2]
        for d in (2, 1, 3):
            second(part, d).start()
    for part, (_, _, (gone, axis, _)) in enumerate(PARTS):
        for d in range(1, 4):
            second(part, d).wait_recv()
        cut = pick([a for a in range(3) if a != gone], axis, at[axis])
        lines[part][...] = sums[part][cut] + twos[part][0] + twos[part][1] + twos[part][2]
        for d in (2, 1, 3):
            third(part, d).start()
    for part, (start, rows, (_, _, axis)) in enumerate(PARTS):
        for d in range(1, 4):
            third(part, d).wait_recv()
        out[0, pl.ds(start, rows)] = lines[part][at[axis]] + threes[part][0] + threes[part][1] + threes[part][2]

    for copy in slot_copies + [share_notes]:
        copy.wait_send()
    for j, step in enumerate(STEPS):
        note(j).wait_send()
        row, to = row_home(step)
        remote(x.at[row], held.at[pl.ds(home * 4, 4)], g_send.at[j], g_recv.at[home], to).wait_send()
    for source in range(8):
        share(source).wait_send()
    for part in range(3):
        for d in range(1, 4):
            first(part, d).wait_send()
            second(part, d).wait_send()
            third(part, d).wait_send()


def per_device(x_tiles, tile_col, keep_mask, out_rows, out_cols):
    vmem, smem = pltpu.VMEM, pltpu.SMEM
    dma = pltpu.SemaphoreType.DMA
    f32, i32 = jnp.float32, jnp.int32
    rows = [part[1] for part in PARTS]
    return pl.pallas_call(
        kernel,
        out_shape=jax.ShapeDtypeStruct((1, 128, 128), f32),
        in_specs=[
            pl.BlockSpec(memory_space=pltpu.HBM),
            pl.BlockSpec(memory_space=pltpu.HBM),
            pl.BlockSpec(memory_space=pltpu.HBM),
            pl.BlockSpec(memory_space=smem),
            pl.BlockSpec(memory_space=smem),
        ],
        out_specs=pl.BlockSpec(memory_space=vmem),
        scratch_shapes=[
            vmem((64, 128, 128), f32),
            vmem((4, 4, 4, 128, 128), f32),
            vmem((4, 8), i32),
            vmem((8, 4, 64), i32),
            vmem((8, 128), i32),
            vmem((8, 8, 128), i32),
            vmem((8, 8, 128), i32),
            vmem((16, 8, 128), i32),
            smem((16, 8, 128), i32),
            smem((64,), i32),
            smem((64,), i32),
            smem((64,), f32),
            *[vmem((3, 4, 4, r, 128), f32) for r in rows],
            *[vmem((3, 4, r, 128), f32) for r in rows],
            *[vmem((3, r, 128), f32) for r in rows],
            *[vmem((4, 4, r, 128), f32) for r in rows],
            *[vmem((4, r, 128), f32) for r in rows],
            dma((4,)), dma((7,)), dma((7,)), dma((7,)), dma((8,)), dma((7,)), dma((8,)),
            dma((8,)), dma((8,)), dma((1,)), dma((1,)), dma((3, 9)), dma((3, 9)),
        ],
        compiler_params=pltpu.CompilerParams(
            collective_id=0, has_side_effects=True, vmem_limit_bytes=59 << 20),
        cost_estimate=pl.CostEstimate(flops=64 * 3 * 2 * 128**3, bytes_accessed=1 << 22, transcendentals=0),
        name="home_product",
    )(x_tiles, tile_col.T, keep_mask.transpose(0, 2, 1), out_rows, out_cols)


def solution(mesh):
    return jax.shard_map(
        per_device,
        mesh=mesh,
        in_specs=(
            P("inner", "cols", None, None),
            P("inner", "cols"),
            P("inner", None, "cols"),
            P(("inner", "cols")),
            P(("inner", "cols")),
        ),
        out_specs=P(("inner", "cols"), None, None),
        check_vma=False,
    )
```

```python
import jax
import jax.numpy as jnp
from jax import lax
from jax.experimental import pallas as pl
from jax.experimental.pallas import tpu as pltpu
from jax.sharding import PartitionSpec as P

MESH = pl.DeviceIdType.MESH
JB_DEV = 60
PARTNERS = 16
STEPS = ((2, 1), (1, 1), (3, 1), (2, 0), (1, 0), (3, 0), (0, 1))
PARTS = ((0, 48, 24, (0, 1, 2)), (48, 40, 24, (1, 2, 0)), (88, 40, 24, (2, 0, 1)))


def kernel(x, tile_col_hbm, keep_hbm, out_row, out_col, out, held, left_top, left_low, right_top, right_low, products, tile_col, keep, mine, slots, notes, heard,
           heard_s, left_s, right_s, gate_s, via_a, via_b, via_c, one_a, one_b, one_c, two_a, two_b, two_c, three_a, three_b, three_c,
           sum_a, sum_b, sum_c, line_a, line_b, line_c,
           local_sem, own_sem, s_send, s_recv, n_send, n_recv, g_send, g_recv, c_send, c_recv, h_send, h_recv, f_send, f_recv,
           r_send, r_recv):
    i = lax.axis_index("inner")
    c = lax.axis_index("cols")
    core = c % 2
    at = (i // 2, c // 4, (i % 2) * 2 + (c // 2) % 2)
    z_hi, z_lo = i % 2, (c // 2) % 2
    home = at[1] * 2 + z_lo

    def device(place, on):
        px, py, pz = place
        return (px * 2 + pz // 2, py * 4 + (pz % 2) * 2 + on)

    def row_home(step):
        py, pz = (at[1] + step[0]) % 4, (z_lo + step[1]) % 2
        return py * 2 + pz, device((at[0], py, z_hi * 2 + pz), core)

    def inner(e):
        return ((i + e) % 8, c)

    def along(axis, d):
        return device(tuple((p + d) % 4 if n == axis else p for n, p in enumerate(at)), core)

    twin = device(at, 1 - core)

    def remote(src, dst, send, recv, to):
        return pltpu.make_async_remote_copy(
            src_ref=src, dst_ref=dst, send_sem=send, recv_sem=recv, device_id=to, device_id_type=MESH)

    load_col = pltpu.make_async_copy(tile_col_hbm, tile_col, local_sem.at[0])
    load_keep = pltpu.make_async_copy(keep_hbm, keep, local_sem.at[1])
    load_col.start()
    load_keep.start()

    def load_own(p):
        return pltpu.make_async_copy(x.at[home, p], held.at[p * 8 + home], own_sem.at[p])

    for p in range(4):
        load_own(p).start()

    barrier = pltpu.get_barrier_semaphore()
    partners = [row_home(step)[1] for step in STEPS] + [inner(e) for e in range(1, 8)]
    partners += [twin, device((at[0], at[1], 3 - at[2]), core)]
    for to in partners:
        pl.semaphore_signal(barrier, inc=1, device_id=to, device_id_type=MESH)

    sublane = lax.broadcasted_iota(jnp.int32, (8, 128), 0)
    lane = lax.broadcasted_iota(jnp.int32, (8, 128), 1)
    mine[...] = jnp.where(sublane == 4, out_row[0], jnp.where(sublane == 5, out_col[0], 0))
    slots[i] = mine[...]
    load_col.wait()
    load_keep.wait()
    pl.semaphore_wait(barrier, PARTNERS)

    slot_copies = [remote(mine, slots.at[i], s_send.at[e - 1], s_recv.at[e - 1], inner(e)) for e in range(1, 8)]
    for copy in slot_copies:
        copy.start()

    def send_blocks(p):
        for j, step in enumerate(STEPS):
            row, to = row_home(step)
            remote(x.at[row, p], held.at[p * 8 + home], g_send.at[j, p], g_recv.at[home, p], to).start()

    send_blocks(0)
    send_blocks(1)
    for copy in slot_copies:
        copy.wait_recv()

    listed = jnp.zeros((8, 128), jnp.int32)
    for s in range(8):
        listed = jnp.where(lane == s, slots[s], listed)
    for k in range(8):
        notes[k] = listed
        notes[k, 0:4, 0:64] = keep[k]
        notes[k, 0:4, 64:128] = jnp.broadcast_to(tile_col[:, k:k + 1], (4, 64))
    heard[home] = notes[home]

    def note(j):
        row, to = row_home(STEPS[j])
        return remote(notes.at[row], heard.at[home], n_send.at[j], n_recv.at[home], to)

    for j in range(7):
        note(j).start()
    send_blocks(2)
    send_blocks(3)

    def share(p):
        return remote(held.at[pl.ds(p * 8, 8)], held.at[pl.ds(32 + p * 8, 8)], c_send.at[p], c_recv.at[p], twin)

    def halves(v):
        top = v.astype(jnp.bfloat16)
        return top, (v - top.astype(jnp.float32)).astype(jnp.bfloat16)

    def prepare_left(n):
        left_top[n], left_low[n] = halves(held[n].T)

    def receive(p):
        for j, step in enumerate(STEPS):
            source, to = row_home(step)
            remote(x.at[0, p], held.at[p * 8 + source], g_send.at[j, p], g_recv.at[source, p], to).wait_recv()
        load_own(p).wait()
        share(p).start()

        def body(n, carry):
            for n in (p * 8 + 2 * n, p * 8 + 2 * n + 1):
                prepare_left(n)
                right_top[n], right_low[n] = halves(held[n])
            return carry

        lax.fori_loop(0, 4, body, 0)

    def receive_shared(p):
        share(p).wait_recv()

        def body(n, carry):
            for n in (p * 8 + 2 * n, p * 8 + 2 * n + 1):
                prepare_left(32 + n)
            return carry

        lax.fori_loop(0, 4, body, 0)

    receive(0)
    receive(1)
    receive_shared(0)
    for j, step in enumerate(STEPS):
        source, to = row_home(step)
        remote(notes.at[0], heard.at[source], n_send.at[j], n_recv.at[source], to).wait_recv()
    share_notes = remote(heard.at[pl.ds(0, 8)], heard.at[pl.ds(8, 8)], h_send.at[0], h_recv.at[0], twin)
    share_notes.start()
    receive_shared(1)
    share_notes.wait_recv()
    stage = pltpu.make_async_copy(heard, heard_s, local_sem.at[2])
    stage.start()
    receive(2)
    stage.wait()

    def find(n):
        sx, sy, sz = n // 16, (n // 4) % 4, n % 4
        index, chip = sx * 2 + sz // 2, sy * 2 + sz % 2
        row, col = heard_s[chip, 4, index], heard_s[chip, 5, index]
        left_slice = row // JB_DEV
        holder = jnp.where(left_slice % 2 == core, 0, 8) + left_slice // 2
        p, q, stored_l, stored_r = jnp.int32(0), jnp.int32(0), jnp.int32(0), jnp.int32(0)
        for r in range(4):
            hit = heard_s[holder, r, 64] == row
            p, stored_l = jnp.where(hit, r, p), jnp.where(hit, 1, stored_l)
            hit = heard_s[chip, r, 64] == col
            q, stored_r = jnp.where(hit, r, q), jnp.where(hit, 1, stored_r)
        left_s[n] = (holder // 8) * 32 + p * 8 + holder % 8
        right_s[n] = q * 8 + chip
        gate_s[n] = (heard_s[chip, q, left_slice * 4 + p] * stored_l * stored_r).astype(jnp.float32)

    def find_some(n, carry):
        for m in range(4):
            find(n * 4 + m)
        return carry

    lax.fori_loop(0, 16, find_some, 0)
    receive_shared(2)
    receive(3)
    receive_shared(3)

    def product(n):
        lt, ll, rt, rl = left_top[left_s[n]], left_low[left_s[n]], right_top[right_s[n]], right_low[right_s[n]]
        return gate_s[n] * (jnp.dot(lt, rt, preferred_element_type=jnp.float32)
                            + jnp.dot(lt, rl, preferred_element_type=jnp.float32)
                            + jnp.dot(ll, rt, preferred_element_type=jnp.float32))

    vias, ones, twos, threes = (via_a, via_b, via_c), (one_a, one_b, one_c), (two_a, two_b, two_c), (three_a, three_b, three_c)
    sums, lines = (sum_a, sum_b, sum_c), (line_a, line_b, line_c)

    def pick(axes_left, axis, where):
        return tuple(where if a == axis else slice(None) for a in axes_left)

    def first(part, way, kind):
        start, rows, split, (axis, _, _) = PARTS[part]
        ahead = 1 if way == 0 else 3
        low, high = (0, split), (split, rows - split)
        begin, count = (low if way == 0 else high) if kind != 1 else (high if way == 0 else low)
        if kind == 2:
            source = vias[part].at[way, :, :, pl.ds(begin, count)]
        else:
            cut = pick((0, 1, 2), axis, (at[axis] + (2 if kind == 0 else ahead)) % 4)
            source = products.at[cut + (pl.ds(start + begin, count),)]
        target = (vias if kind == 0 else ones)[part].at[way, :, :, pl.ds(begin, count)]
        n = way * 3 + kind
        return remote(source, target, f_send.at[part, n], f_recv.at[part, n], along(axis, ahead))

    def add_own(part, way):
        start, rows, split, (axis, _, _) = PARTS[part]
        first(part, way, 0).wait_recv()
        begin, count = (0, split) if way == 0 else (split, rows - split)

        def body(n, carry):
            cut = pick((0, 1, 2), axis, (at[axis] + 1 + 2 * way) % 4)
            one = [n if isinstance(a, slice) else a for a in cut]
            free = [j for j, a in enumerate(cut) if isinstance(a, slice)]
            one[free[0]], one[free[1]] = n // 4, n % 4
            rows_there = pl.ds(start + begin, count)
            here = (way, n // 4, n % 4, pl.ds(begin, count))
            vias[part][here] = vias[part][here] + products[tuple(one) + (rows_there,)]
            return carry

        lax.fori_loop(0, 16, body, 0)
        first(part, way, 2).start()

    def second(part, d):
        _, _, _, (gone, axis, _) = PARTS[part]
        cut = pick([a for a in range(3) if a != gone], axis, (at[axis] + d) % 4)
        return remote(sums[part].at[cut], twos[part].at[d - 1], r_send.at[part, d - 1], r_recv.at[part, d - 1], along(axis, d))

    def third(part, d):
        _, _, _, (_, _, axis) = PARTS[part]
        return remote(lines[part].at[(at[axis] + d) % 4], threes[part].at[d - 1],
                      r_send.at[part, 2 + d], r_recv.at[part, 2 + d], along(axis, d))

    def slab(j, carry):
        px = (at[0] + jnp.where(j < 2, 2 + j, 3 - j)) % 4

        def body(n, carry):
            for m in range(4):
                products[px, n, m] = product(px * 16 + n * 4 + m)
            return carry

        lax.fori_loop(0, 4, body, 0)

        @pl.when(j == 0)
        def _():
            first(0, 0, 0).start()
            first(0, 1, 0).start()

        @pl.when(j == 1)
        def _():
            first(0, 1, 1).start()

        @pl.when(j == 2)
        def _():
            first(0, 0, 1).start()

        return carry

    lax.fori_loop(0, 4, slab, 0)
    for kind in range(2):
        for part in (1, 2):
            for way in range(2):
                first(part, way, kind).start()
    for part in range(3):
        for way in range(2):
            add_own(part, way)

    for part, (start, rows, _, (axis, _, _)) in enumerate(PARTS):
        for way in range(2):
            first(part, way, 1).wait_recv()
            first(part, way, 2).wait_recv()

        def total(n, carry):
            cut = pick((0, 1, 2), axis, at[axis])
            one, free = list(cut), [j for j, a in enumerate(cut) if isinstance(a, slice)]
            one[free[0]], one[free[1]] = n // 4, n % 4
            sums[part][n // 4, n % 4] = (products[tuple(one) + (pl.ds(start, rows),)]
                                         + ones[part][0, n // 4, n % 4] + ones[part][1, n // 4, n % 4])
            return carry

        lax.fori_loop(0, 16, total, 0)
        for d in (2, 1, 3):
            second(part, d).start()
    for part, (_, _, _, (gone, axis, _)) in enumerate(PARTS):
        for d in range(1, 4):
            second(part, d).wait_recv()
        cut = pick([a for a in range(3) if a != gone], axis, at[axis])
        lines[part][...] = sums[part][cut] + twos[part][0] + twos[part][1] + twos[part][2]
        for d in (2, 1, 3):
            third(part, d).start()
    for part, (start, rows, _, (_, _, axis)) in enumerate(PARTS):
        for d in range(1, 4):
            third(part, d).wait_recv()
        out[0, pl.ds(start, rows)] = lines[part][at[axis]] + threes[part][0] + threes[part][1] + threes[part][2]

    for copy in slot_copies + [share_notes]:
        copy.wait_send()
    for j, step in enumerate(STEPS):
        note(j).wait_send()
        row, to = row_home(step)
        for p in range(4):
            remote(x.at[row, p], held.at[p * 8 + home], g_send.at[j, p], g_recv.at[home, p], to).wait_send()
    for p in range(4):
        share(p).wait_send()
    for part in range(3):
        for d in range(1, 4):
            second(part, d).wait_send()
            third(part, d).wait_send()
        for way in range(2):
            for kind in range(3):
                first(part, way, kind).wait_send()


def per_device(x_tiles, tile_col, keep_mask, out_rows, out_cols):
    vmem, smem = pltpu.VMEM, pltpu.SMEM
    dma = pltpu.SemaphoreType.DMA
    f32, i32 = jnp.float32, jnp.int32
    rows = [part[1] for part in PARTS]
    return pl.pallas_call(
        kernel,
        out_shape=jax.ShapeDtypeStruct((1, 128, 128), f32),
        in_specs=[
            pl.BlockSpec(memory_space=pltpu.HBM),
            pl.BlockSpec(memory_space=pltpu.HBM),
            pl.BlockSpec(memory_space=pltpu.HBM),
            pl.BlockSpec(memory_space=smem),
            pl.BlockSpec(memory_space=smem),
        ],
        out_specs=pl.BlockSpec(memory_space=vmem),
        scratch_shapes=[
            vmem((64, 128, 128), f32),
            vmem((64, 128, 128), jnp.bfloat16),
            vmem((64, 128, 128), jnp.bfloat16),
            vmem((32, 128, 128), jnp.bfloat16),
            vmem((32, 128, 128), jnp.bfloat16),
            vmem((4, 4, 4, 128, 128), f32),
            vmem((4, 8), i32),
            vmem((8, 4, 64), i32),
            vmem((8, 128), i32),
            vmem((8, 8, 128), i32),
            vmem((8, 8, 128), i32),
            vmem((16, 8, 128), i32),
            smem((16, 8, 128), i32),
            smem((64,), i32),
            smem((64,), i32),
            smem((64,), f32),
            *[vmem((2, 4, 4, r, 128), f32) for r in rows],
            *[vmem((2, 4, 4, r, 128), f32) for r in rows],
            *[vmem((3, 4, r, 128), f32) for r in rows],
            *[vmem((3, r, 128), f32) for r in rows],
            *[vmem((4, 4, r, 128), f32) for r in rows],
            *[vmem((4, r, 128), f32) for r in rows],
            dma((3,)), dma((4,)), dma((7,)), dma((7,)), dma((7,)), dma((8,)), dma((7, 4)), dma((8, 4)),
            dma((4,)), dma((4,)), dma((1,)), dma((1,)), dma((3, 6)), dma((3, 6)), dma((3, 6)), dma((3, 6)),
        ],
        compiler_params=pltpu.CompilerParams(
            collective_id=0, has_side_effects=True, vmem_limit_bytes=59 << 20),
        cost_estimate=pl.CostEstimate(flops=64 * 3 * 2 * 128**3, bytes_accessed=1 << 22, transcendentals=0),
        name="home_product",
    )(x_tiles, tile_col.T, keep_mask.transpose(0, 2, 1), out_rows, out_cols)


def solution(mesh):
    return jax.shard_map(
        per_device,
        mesh=mesh,
        in_specs=(
            P("inner", "cols", None, None),
            P("inner", "cols"),
            P("inner", None, "cols"),
            P(("inner", "cols")),
            P(("inner", "cols")),
        ),
        out_specs=P(("inner", "cols"), None, None),
        check_vma=False,
    )
```

```python
import jax
import jax.numpy as jnp
from jax import lax
from jax.experimental import pallas as pl
from jax.experimental.pallas import tpu as pltpu
from jax.sharding import PartitionSpec as P

MESH = pl.DeviceIdType.MESH
JB_DEV = 60
PARTNERS = 16
STEPS = ((2, 1), (1, 1), (3, 1), (2, 0), (1, 0), (3, 0), (0, 1))
PARTS = (
    (0, 24, 16, (0, 1, 2)), (48, 24, 16, (1, 2, 0)), (88, 24, 16, (2, 0, 1)),
    (24, 24, 8, (0, 1, 2)), (72, 16, 8, (1, 2, 0)), (112, 16, 8, (2, 0, 1)),
)
HALVES = ((0, 1, 2), (3, 4, 5))


def kernel(x, tile_col_hbm, keep_hbm, out_row, out_col, out, held, left_top, left_low, right_top, right_low, products,
           tile_col, keep, mine, slots, notes, heard, heard_s, left_s, right_s, gate_s, *rest):
    vias, ones, twos, threes, sums, lines = (rest[6 * n:6 * n + 6] for n in range(6))
    (local_sem, own_sem, s_send, s_recv, n_send, n_recv, g_send, g_recv, c_send, c_recv, h_send, h_recv,
     f_send, f_recv, r_send, r_recv) = rest[36:]
    i = lax.axis_index("inner")
    c = lax.axis_index("cols")
    core = c % 2
    at = (i // 2, c // 4, (i % 2) * 2 + (c // 2) % 2)
    z_hi, z_lo = i % 2, (c // 2) % 2
    home = at[1] * 2 + z_lo

    def device(place, on):
        px, py, pz = place
        return (px * 2 + pz // 2, py * 4 + (pz % 2) * 2 + on)

    def row_home(step):
        py, pz = (at[1] + step[0]) % 4, (z_lo + step[1]) % 2
        return py * 2 + pz, device((at[0], py, z_hi * 2 + pz), core)

    def inner(e):
        return ((i + e) % 8, c)

    def along(axis, d):
        return device(tuple((p + d) % 4 if n == axis else p for n, p in enumerate(at)), core)

    twin = device(at, 1 - core)

    def remote(src, dst, send, recv, to):
        return pltpu.make_async_remote_copy(
            src_ref=src, dst_ref=dst, send_sem=send, recv_sem=recv, device_id=to, device_id_type=MESH)

    load_col = pltpu.make_async_copy(tile_col_hbm, tile_col, local_sem.at[0])
    load_keep = pltpu.make_async_copy(keep_hbm, keep, local_sem.at[1])
    load_col.start()
    load_keep.start()

    def load_own(p):
        return pltpu.make_async_copy(x.at[home, p], held.at[p * 8 + home], own_sem.at[p])

    for p in range(4):
        load_own(p).start()

    barrier = pltpu.get_barrier_semaphore()
    partners = [row_home(step)[1] for step in STEPS] + [inner(e) for e in range(1, 8)]
    partners += [twin, device((at[0], at[1], 3 - at[2]), core)]
    for to in partners:
        pl.semaphore_signal(barrier, inc=1, device_id=to, device_id_type=MESH)

    sublane = lax.broadcasted_iota(jnp.int32, (8, 128), 0)
    lane = lax.broadcasted_iota(jnp.int32, (8, 128), 1)
    mine[...] = jnp.where(sublane == 4, out_row[0], jnp.where(sublane == 5, out_col[0], 0))
    slots[i] = mine[...]
    load_col.wait()
    load_keep.wait()
    pl.semaphore_wait(barrier, PARTNERS)

    slot_copies = [remote(mine, slots.at[i], s_send.at[e - 1], s_recv.at[e - 1], inner(e)) for e in range(1, 8)]
    for copy in slot_copies:
        copy.start()

    def send_blocks(p):
        for j, step in enumerate(STEPS):
            row, to = row_home(step)
            remote(x.at[row, p], held.at[p * 8 + home], g_send.at[j, p], g_recv.at[home, p], to).start()

    send_blocks(0)
    send_blocks(1)
    for copy in slot_copies:
        copy.wait_recv()

    listed = jnp.zeros((8, 128), jnp.int32)
    for s in range(8):
        listed = jnp.where(lane == s, slots[s], listed)
    for k in range(8):
        notes[k] = listed
        notes[k, 0:4, 0:64] = keep[k]
        notes[k, 0:4, 64:128] = jnp.broadcast_to(tile_col[:, k:k + 1], (4, 64))
    heard[home] = notes[home]

    def note(j):
        row, to = row_home(STEPS[j])
        return remote(notes.at[row], heard.at[home], n_send.at[j], n_recv.at[home], to)

    for j in range(7):
        note(j).start()
    send_blocks(2)
    send_blocks(3)

    def share(p):
        return remote(held.at[pl.ds(p * 8, 8)], held.at[pl.ds(32 + p * 8, 8)], c_send.at[p], c_recv.at[p], twin)

    def halves(v):
        top = v.astype(jnp.bfloat16)
        return top, (v - top.astype(jnp.float32)).astype(jnp.bfloat16)

    def prepare_left(n):
        left_top[n], left_low[n] = halves(held[n].T)

    def receive(p):
        for j, step in enumerate(STEPS):
            source, to = row_home(step)
            remote(x.at[0, p], held.at[p * 8 + source], g_send.at[j, p], g_recv.at[source, p], to).wait_recv()
        load_own(p).wait()
        share(p).start()

        def body(n, carry):
            for n in (p * 8 + 2 * n, p * 8 + 2 * n + 1):
                prepare_left(n)
                right_top[n], right_low[n] = halves(held[n])
            return carry

        lax.fori_loop(0, 4, body, 0)

    def receive_shared(p):
        share(p).wait_recv()

        def body(n, carry):
            for n in (p * 8 + 2 * n, p * 8 + 2 * n + 1):
                prepare_left(32 + n)
            return carry

        lax.fori_loop(0, 4, body, 0)

    receive(0)
    receive(1)
    receive_shared(0)
    for j, step in enumerate(STEPS):
        source, to = row_home(step)
        remote(notes.at[0], heard.at[source], n_send.at[j], n_recv.at[source], to).wait_recv()
    share_notes = remote(heard.at[pl.ds(0, 8)], heard.at[pl.ds(8, 8)], h_send.at[0], h_recv.at[0], twin)
    share_notes.start()
    receive_shared(1)
    share_notes.wait_recv()
    stage = pltpu.make_async_copy(heard, heard_s, local_sem.at[2])
    stage.start()
    receive(2)
    stage.wait()

    def find(n):
        sx, sy, sz = n // 16, (n // 4) % 4, n % 4
        index, chip = sx * 2 + sz // 2, sy * 2 + sz % 2
        row, col = heard_s[chip, 4, index], heard_s[chip, 5, index]
        left_slice = row // JB_DEV
        holder = jnp.where(left_slice % 2 == core, 0, 8) + left_slice // 2
        p, q, stored_l, stored_r = jnp.int32(0), jnp.int32(0), jnp.int32(0), jnp.int32(0)
        for r in range(4):
            hit = heard_s[holder, r, 64] == row
            p, stored_l = jnp.where(hit, r, p), jnp.where(hit, 1, stored_l)
            hit = heard_s[chip, r, 64] == col
            q, stored_r = jnp.where(hit, r, q), jnp.where(hit, 1, stored_r)
        left_s[n] = (holder // 8) * 32 + p * 8 + holder % 8
        right_s[n] = q * 8 + chip
        gate_s[n] = (heard_s[chip, q, left_slice * 4 + p] * stored_l * stored_r).astype(jnp.float32)

    def find_some(n, carry):
        for m in range(4):
            find(n * 4 + m)
        return carry

    lax.fori_loop(0, 16, find_some, 0)
    receive_shared(2)
    receive(3)
    receive_shared(3)

    def product(n):
        lt, ll, rt, rl = left_top[left_s[n]], left_low[left_s[n]], right_top[right_s[n]], right_low[right_s[n]]
        return gate_s[n] * (jnp.dot(lt, rt, preferred_element_type=jnp.float32)
                            + jnp.dot(lt, rl, preferred_element_type=jnp.float32)
                            + jnp.dot(ll, rt, preferred_element_type=jnp.float32))

    def pick(axes_left, axis, where):
        return tuple(where if a == axis else slice(None) for a in axes_left)

    def first(part, way, kind):
        start, rows, split, (axis, _, _) = PARTS[part]
        ahead = 1 if way == 0 else 3
        low, high = (0, split), (split, rows - split)
        begin, count = (low if way == 0 else high) if kind != 1 else (high if way == 0 else low)
        if kind == 2:
            source = vias[part].at[way, :, :, pl.ds(begin, count)]
        else:
            cut = pick((0, 1, 2), axis, (at[axis] + (2 if kind == 0 else ahead)) % 4)
            source = products.at[cut + (pl.ds(start + begin, count),)]
        target = (vias if kind == 0 else ones)[part].at[way, :, :, pl.ds(begin, count)]
        n = way * 3 + kind
        return remote(source, target, f_send.at[part, n], f_recv.at[part, n], along(axis, ahead))

    def add_own(part, way):
        start, rows, split, (axis, _, _) = PARTS[part]
        first(part, way, 0).wait_recv()
        begin, count = (0, split) if way == 0 else (split, rows - split)

        cut = pick((0, 1, 2), axis, (at[axis] + 1 + 2 * way) % 4)
        free = [j for j, a in enumerate(cut) if isinstance(a, slice)]

        def body(n, carry):
            one = list(cut)
            one[free[0]] = n
            here = (way, n, slice(None), pl.ds(begin, count))
            vias[part][here] = vias[part][here] + products[tuple(one) + (pl.ds(start + begin, count),)]
            return carry

        lax.fori_loop(0, 4, body, 0)
        first(part, way, 2).start()

    def second(part, d):
        _, _, _, (gone, axis, _) = PARTS[part]
        cut = pick([a for a in range(3) if a != gone], axis, (at[axis] + d) % 4)
        return remote(sums[part].at[cut], twos[part].at[d - 1], r_send.at[part, d - 1], r_recv.at[part, d - 1], along(axis, d))

    def third(part, d):
        _, _, _, (_, _, axis) = PARTS[part]
        return remote(lines[part].at[(at[axis] + d) % 4], threes[part].at[d - 1],
                      r_send.at[part, 2 + d], r_recv.at[part, 2 + d], along(axis, d))

    def slab(j, carry):
        px = (at[0] + jnp.where(j < 2, 2 + j, 3 - j)) % 4

        def body(n, carry):
            for m in range(8):
                products[px, 2 * n + m // 4, m % 4] = product(px * 16 + n * 8 + m)
            return carry

        lax.fori_loop(0, 2, body, 0)

        @pl.when(j == 0)
        def _():
            first(0, 0, 0).start()
            first(0, 1, 0).start()

        @pl.when(j == 1)
        def _():
            first(0, 1, 1).start()

        @pl.when(j == 2)
        def _():
            first(0, 0, 1).start()

        return carry

    lax.fori_loop(0, 4, slab, 0)
    def both_ways(part, kind):
        for way in range(2):
            first(part, way, kind).start()

    for part, kind in ((1, 0), (2, 0), (1, 1), (2, 1), (3, 0), (4, 0), (5, 0)):
        both_ways(part, kind)
    for part in HALVES[0]:
        for way in range(2):
            add_own(part, way)
    for part in HALVES[1]:
        both_ways(part, 1)
    for part in HALVES[1]:
        for way in range(2):
            add_own(part, way)

    for part, (start, rows, _, (axis, _, _)) in enumerate(PARTS):
        for way in range(2):
            first(part, way, 1).wait_recv()
            first(part, way, 2).wait_recv()

        cut = pick((0, 1, 2), axis, at[axis])
        free = [j for j, a in enumerate(cut) if isinstance(a, slice)]

        def total(n, carry):
            one = list(cut)
            one[free[0]] = n
            sums[part][n] = products[tuple(one) + (pl.ds(start, rows),)] + ones[part][0, n] + ones[part][1, n]
            return carry

        lax.fori_loop(0, 4, total, 0)
        for d in (2, 1, 3):
            second(part, d).start()
    for part, (_, _, _, (gone, axis, _)) in enumerate(PARTS):
        for d in range(1, 4):
            second(part, d).wait_recv()
        cut = pick([a for a in range(3) if a != gone], axis, at[axis])
        lines[part][...] = sums[part][cut] + twos[part][0] + twos[part][1] + twos[part][2]
        for d in (2, 1, 3):
            third(part, d).start()
    for part, (start, rows, _, (_, _, axis)) in enumerate(PARTS):
        for d in range(1, 4):
            third(part, d).wait_recv()
        out[0, pl.ds(start, rows)] = lines[part][at[axis]] + threes[part][0] + threes[part][1] + threes[part][2]

    for copy in slot_copies + [share_notes]:
        copy.wait_send()
    for j, step in enumerate(STEPS):
        note(j).wait_send()
        row, to = row_home(step)
        for p in range(4):
            remote(x.at[row, p], held.at[p * 8 + home], g_send.at[j, p], g_recv.at[home, p], to).wait_send()
    for p in range(4):
        share(p).wait_send()
    for part in range(6):
        for d in range(1, 4):
            second(part, d).wait_send()
            third(part, d).wait_send()
        for way in range(2):
            for kind in range(3):
                first(part, way, kind).wait_send()


def per_device(x_tiles, tile_col, keep_mask, out_rows, out_cols):
    vmem, smem = pltpu.VMEM, pltpu.SMEM
    dma = pltpu.SemaphoreType.DMA
    f32, i32 = jnp.float32, jnp.int32
    rows = [part[1] for part in PARTS]
    return pl.pallas_call(
        kernel,
        out_shape=jax.ShapeDtypeStruct((1, 128, 128), f32),
        in_specs=[
            pl.BlockSpec(memory_space=pltpu.HBM),
            pl.BlockSpec(memory_space=pltpu.HBM),
            pl.BlockSpec(memory_space=pltpu.HBM),
            pl.BlockSpec(memory_space=smem),
            pl.BlockSpec(memory_space=smem),
        ],
        out_specs=pl.BlockSpec(memory_space=vmem),
        scratch_shapes=[
            vmem((64, 128, 128), f32),
            vmem((64, 128, 128), jnp.bfloat16),
            vmem((64, 128, 128), jnp.bfloat16),
            vmem((32, 128, 128), jnp.bfloat16),
            vmem((32, 128, 128), jnp.bfloat16),
            vmem((4, 4, 4, 128, 128), f32),
            vmem((4, 8), i32),
            vmem((8, 4, 64), i32),
            vmem((8, 128), i32),
            vmem((8, 8, 128), i32),
            vmem((8, 8, 128), i32),
            vmem((16, 8, 128), i32),
            smem((16, 8, 128), i32),
            smem((64,), i32),
            smem((64,), i32),
            smem((64,), f32),
            *[vmem((2, 4, 4, r, 128), f32) for r in rows],
            *[vmem((2, 4, 4, r, 128), f32) for r in rows],
            *[vmem((3, 4, r, 128), f32) for r in rows],
            *[vmem((3, r, 128), f32) for r in rows],
            *[vmem((4, 4, r, 128), f32) for r in rows],
            *[vmem((4, r, 128), f32) for r in rows],
            dma((3,)), dma((4,)), dma((7,)), dma((7,)), dma((7,)), dma((8,)), dma((7, 4)), dma((8, 4)),
            dma((4,)), dma((4,)), dma((1,)), dma((1,)), dma((6, 6)), dma((6, 6)), dma((6, 6)), dma((6, 6)),
        ],
        compiler_params=pltpu.CompilerParams(
            collective_id=0, has_side_effects=True, vmem_limit_bytes=40 << 20),
        cost_estimate=pl.CostEstimate(flops=64 * 3 * 2 * 128**3, bytes_accessed=1 << 22, transcendentals=0),
        name="home_product",
    )(*(pltpu.with_memory_space_constraint(a, pltpu.HBM) for a in (x_tiles, tile_col.T, keep_mask.transpose(0, 2, 1))), out_rows, out_cols)


def solution(mesh):
    return jax.shard_map(
        per_device,
        mesh=mesh,
        in_specs=(
            P("inner", "cols", None, None),
            P("inner", "cols"),
            P("inner", None, "cols"),
            P(("inner", "cols")),
            P(("inner", "cols")),
        ),
        out_specs=P(("inner", "cols"), None, None),
        check_vma=False,
    )
```

```python
import jax
import jax.numpy as jnp
from jax import lax
from jax.experimental import pallas as pl
from jax.experimental.pallas import tpu as pltpu
from jax.sharding import PartitionSpec as P

MESH = pl.DeviceIdType.MESH
JB_DEV = 60
PARTNERS = 16
STEPS = ((0, 1), (1, 0), (3, 0), (1, 1), (3, 1), (2, 0), (2, 1))
PARTS = ((0, 32, 16, (0, 1, 2)), (48, 24, 16, (1, 2, 0)), (88, 24, 8, (2, 0, 1)), (32, 16, 8, (0, 1, 2)), (72, 16, 8, (1, 2, 0)), (112, 16, 8, (2, 0, 1)))
HALVES = ((0, 1, 2), (3, 4, 5))


def kernel(x, tile_col_hbm, keep_hbm, out_row, out_col, out, held, left_top, left_low, right_top, right_low, products,
           tile_col, keep, mine, slots, notes, heard, heard_s, left_s, right_s, gate_s, *rest):
    vias, ones, twos, sums = (rest[6 * n:6 * n + 6] for n in range(4))
    threes, lines = rest[24:27], rest[27:30]
    (local_sem, own_sem, s_send, s_recv, n_send, n_recv, g_send, g_recv, c_send, c_recv, h_send, h_recv,
     f_send, f_recv, r_send, r_recv) = rest[30:]
    i = lax.axis_index("inner")
    c = lax.axis_index("cols")
    core = c % 2
    at = (i // 2, c // 4, (i % 2) * 2 + (c // 2) % 2)
    z_hi, z_lo = i % 2, (c // 2) % 2
    home = at[1] * 2 + z_lo

    def device(place, on):
        px, py, pz = place
        return (px * 2 + pz // 2, py * 4 + (pz % 2) * 2 + on)

    def row_home(step):
        py, pz = (at[1] + step[0]) % 4, (z_lo + step[1]) % 2
        return py * 2 + pz, device((at[0], py, z_hi * 2 + pz), core)

    def inner(e):
        return ((i + e) % 8, c)

    def along(axis, d):
        return device(tuple((p + d) % 4 if n == axis else p for n, p in enumerate(at)), core)

    twin = device(at, 1 - core)

    def remote(src, dst, send, recv, to):
        return pltpu.make_async_remote_copy(
            src_ref=src, dst_ref=dst, send_sem=send, recv_sem=recv, device_id=to, device_id_type=MESH)

    load_col = pltpu.make_async_copy(tile_col_hbm, tile_col, local_sem.at[0])
    load_keep = pltpu.make_async_copy(keep_hbm, keep, local_sem.at[1])
    load_col.start()
    load_keep.start()

    def load_own(p):
        return pltpu.make_async_copy(x.at[home, p], held.at[p * 8 + home], own_sem.at[p])

    for p in range(4):
        load_own(p).start()

    barrier = pltpu.get_barrier_semaphore()
    partners = [row_home(step)[1] for step in STEPS] + [inner(e) for e in range(1, 8)]
    partners += [twin, device((at[0], at[1], 3 - at[2]), core)]
    for to in partners:
        pl.semaphore_signal(barrier, inc=1, device_id=to, device_id_type=MESH)

    sublane = lax.broadcasted_iota(jnp.int32, (8, 128), 0)
    lane = lax.broadcasted_iota(jnp.int32, (8, 128), 1)
    mine[...] = jnp.where(sublane == 4, out_row[0], jnp.where(sublane == 5, out_col[0], 0))
    slots[i] = mine[...]
    load_col.wait()
    load_keep.wait()
    pl.semaphore_wait(barrier, PARTNERS)

    slot_copies = [remote(mine, slots.at[i], s_send.at[e - 1], s_recv.at[e - 1], inner(e)) for e in range(1, 8)]
    def send_blocks(p):
        for j, step in enumerate(STEPS):
            row, to = row_home(step)
            remote(x.at[row, p], held.at[p * 8 + home], g_send.at[j, p], g_recv.at[home, p], to).start()

    send_blocks(0)
    for copy in slot_copies:
        copy.start()
    send_blocks(1)
    for copy in slot_copies:
        copy.wait_recv()

    listed = jnp.zeros((8, 128), jnp.int32)
    for s in range(8):
        listed = jnp.where(lane == s, slots[s], listed)
    for k in range(8):
        notes[k] = listed
        notes[k, 0:4, 0:64] = keep[k]
        notes[k, 0:4, 64:128] = jnp.broadcast_to(tile_col[:, k:k + 1], (4, 64))
    heard[home] = notes[home]

    def note(j):
        row, to = row_home(STEPS[j])
        return remote(notes.at[row], heard.at[home], n_send.at[j], n_recv.at[home], to)

    for j in range(7):
        note(j).start()
    send_blocks(2)
    send_blocks(3)

    def share(p):
        return remote(held.at[pl.ds(p * 8, 8)], held.at[pl.ds(32 + p * 8, 8)], c_send.at[p], c_recv.at[p], twin)

    def halves(v):
        top = v.astype(jnp.bfloat16)
        return top, (v - top.astype(jnp.float32)).astype(jnp.bfloat16)

    def prepare_left(n):
        left_top[n], left_low[n] = halves(held[n].T)

    def receive(p):
        for j, step in enumerate(STEPS):
            source, to = row_home(step)
            remote(x.at[0, p], held.at[p * 8 + source], g_send.at[j, p], g_recv.at[source, p], to).wait_recv()
        load_own(p).wait()
        share(p).start()

        for n in range(p * 8, p * 8 + 8):
            prepare_left(n)
            right_top[n], right_low[n] = halves(held[n])

    def receive_shared(p):
        share(p).wait_recv()

        for n in range(p * 8, p * 8 + 8):
            prepare_left(32 + n)

    receive(0)
    receive(1)
    receive_shared(0)
    for j, step in enumerate(STEPS):
        source, to = row_home(step)
        remote(notes.at[0], heard.at[source], n_send.at[j], n_recv.at[source], to).wait_recv()
    share_notes = remote(heard.at[pl.ds(0, 8)], heard.at[pl.ds(8, 8)], h_send.at[0], h_recv.at[0], twin)
    share_notes.start()
    receive_shared(1)
    share_notes.wait_recv()
    stage = pltpu.make_async_copy(heard, heard_s, local_sem.at[2])
    stage.start()
    stage.wait()

    def find(n):
        sx, sy, sz = n // 16, (n // 4) % 4, n % 4
        index, chip = sx * 2 + sz // 2, sy * 2 + sz % 2
        row, col = heard_s[chip, 4, index], heard_s[chip, 5, index]
        left_slice = row // JB_DEV
        holder = jnp.where(left_slice % 2 == core, 0, 8) + left_slice // 2
        p, q, stored_l, stored_r = jnp.int32(0), jnp.int32(0), jnp.int32(0), jnp.int32(0)
        for r in range(4):
            hit = heard_s[holder, r, 64] == row
            p, stored_l = jnp.where(hit, r, p), jnp.where(hit, 1, stored_l)
            hit = heard_s[chip, r, 64] == col
            q, stored_r = jnp.where(hit, r, q), jnp.where(hit, 1, stored_r)
        left_s[n] = (holder // 8) * 32 + p * 8 + holder % 8
        right_s[n] = q * 8 + chip
        gate_s[n] = (heard_s[chip, q, left_slice * 4 + p] * stored_l * stored_r).astype(jnp.float32)

    def find_some(n, carry):
        for m in range(4):
            find(n * 4 + m)
        return carry

    lax.fori_loop(0, 16, find_some, 0)
    receive(2)
    receive_shared(2)
    receive(3)
    receive_shared(3)

    def product(n):
        lt, ll, rt, rl = left_top[left_s[n]], left_low[left_s[n]], right_top[right_s[n]], right_low[right_s[n]]
        return gate_s[n] * (jnp.dot(lt, rt, preferred_element_type=jnp.float32)
                            + jnp.dot(lt, rl, preferred_element_type=jnp.float32)
                            + jnp.dot(ll, rt, preferred_element_type=jnp.float32))

    def pick(axes_left, axis, where):
        return tuple(where if a == axis else slice(None) for a in axes_left)

    def first(part, way, kind):
        start, rows, split, (axis, _, _) = PARTS[part]
        ahead = 1 if way == 0 else 3
        low, high = (0, split), (split, rows - split)
        begin, count = (low if way == 0 else high) if kind != 1 else (high if way == 0 else low)
        if kind == 2:
            source = vias[part].at[way, :, :, pl.ds(begin, count)]
        else:
            cut = pick((0, 1, 2), axis, (at[axis] + (2 if kind == 0 else ahead)) % 4)
            source = products.at[cut + (pl.ds(start + begin, count),)]
        target = (vias if kind == 0 else ones)[part].at[way, :, :, pl.ds(begin, count)]
        n = way * 3 + kind
        return remote(source, target, f_send.at[part, n], f_recv.at[part, n], along(axis, ahead))

    def add_own(part, way):
        start, rows, split, (axis, _, _) = PARTS[part]
        first(part, way, 0).wait_recv()
        begin, count = (0, split) if way == 0 else (split, rows - split)

        cut = pick((0, 1, 2), axis, (at[axis] + 1 + 2 * way) % 4)
        free = [j for j, a in enumerate(cut) if isinstance(a, slice)]

        def body(n, carry):
            one = list(cut)
            one[free[0]] = n
            here = (way, n, slice(None), pl.ds(begin, count))
            vias[part][here] = vias[part][here] + products[tuple(one) + (pl.ds(start + begin, count),)]
            return carry

        lax.fori_loop(0, 4, body, 0)
        first(part, way, 2).start()

    def second(part, d):
        _, _, _, (gone, axis, _) = PARTS[part]
        cut = pick([a for a in range(3) if a != gone], axis, (at[axis] + d) % 4)
        return remote(sums[part].at[cut], twos[part].at[d - 1], r_send.at[part, d - 1], r_recv.at[part, d - 1], along(axis, d))

    def third(order, d):
        axis = PARTS[order][3][2]
        return remote(lines[order].at[(at[axis] + d) % 4], threes[order].at[d - 1],
                      r_send.at[order, 2 + d], r_recv.at[order, 2 + d], along(axis, d))

    def slab(j, carry):
        px = (at[0] + jnp.where(j < 2, 2 + j, 3 - j)) % 4

        for m in range(16):
            products[px, m // 4, m % 4] = product(px * 16 + m)

        @pl.when(j == 0)
        def _():
            first(0, 0, 0).start()
            first(0, 1, 0).start()

        @pl.when(j == 1)
        def _():
            first(0, 1, 1).start()

        @pl.when(j == 2)
        def _():
            first(0, 0, 1).start()

        return carry

    lax.fori_loop(0, 4, slab, 0)
    def both_ways(part, kind):
        for way in range(2):
            first(part, way, kind).start()

    for part, kind in ((1, 0), (2, 0), (1, 1), (2, 1), (3, 0), (4, 0), (5, 0)):
        both_ways(part, kind)
    for copy in slot_copies + [share_notes]:
        copy.wait_send()
    for j, step in enumerate(STEPS):
        note(j).wait_send()
        row, to = row_home(step)
        for p in range(4):
            remote(x.at[row, p], held.at[p * 8 + home], g_send.at[j, p], g_recv.at[home, p], to).wait_send()
    for p in range(4):
        share(p).wait_send()
    for part in HALVES[0]:
        for way in range(2):
            add_own(part, way)
    for part in HALVES[1]:
        both_ways(part, 1)
    for part in HALVES[1]:
        for way in range(2):
            add_own(part, way)

    for part, (start, rows, _, (axis, _, _)) in enumerate(PARTS):
        for way in range(2):
            first(part, way, 1).wait_recv()
            first(part, way, 2).wait_recv()

        cut = pick((0, 1, 2), axis, at[axis])
        free = [j for j, a in enumerate(cut) if isinstance(a, slice)]

        def total(n, carry):
            one = list(cut)
            one[free[0]] = n
            sums[part][n] = products[tuple(one) + (pl.ds(start, rows),)] + ones[part][0, n] + ones[part][1, n]
            return carry

        lax.fori_loop(0, 4, total, 0)
        for d in (2, 1, 3):
            second(part, d).start()
    for part in range(6):
        for way in range(2):
            for kind in range(3):
                first(part, way, kind).wait_send()
    for part in (0, 3, 1, 4, 2, 5):
        _, rows, _, (gone, axis, _) = PARTS[part]
        order, inside = part % 3, (PARTS[part][0] - PARTS[part % 3][0])
        for d in range(1, 4):
            second(part, d).wait_recv()
        cut = pick([a for a in range(3) if a != gone], axis, at[axis])
        lines[order][:, pl.ds(inside, rows)] = sums[part][cut] + twos[part][0] + twos[part][1] + twos[part][2]
        if part > 2:
            for d in (2, 1, 3):
                third(order, d).start()
    for part in range(6):
        for d in range(1, 4):
            second(part, d).wait_send()
    for order in range(3):
        start, rows, axis = PARTS[order][0], PARTS[order][1] + PARTS[order + 3][1], PARTS[order][3][2]
        for d in range(1, 4):
            third(order, d).wait_recv()
        out[0, pl.ds(start, rows)] = lines[order][at[axis]] + threes[order][0] + threes[order][1] + threes[order][2]

    for order in range(3):
        for d in range(1, 4):
            third(order, d).wait_send()


def per_device(x_tiles, tile_col, keep_mask, out_rows, out_cols):
    vmem, smem = pltpu.VMEM, pltpu.SMEM
    dma = pltpu.SemaphoreType.DMA
    f32, i32 = jnp.float32, jnp.int32
    rows = [part[1] for part in PARTS]
    return pl.pallas_call(
        kernel,
        out_shape=jax.ShapeDtypeStruct((1, 128, 128), f32),
        in_specs=[
            pl.BlockSpec(memory_space=pltpu.HBM),
            pl.BlockSpec(memory_space=pltpu.HBM),
            pl.BlockSpec(memory_space=pltpu.HBM),
            pl.BlockSpec(memory_space=smem),
            pl.BlockSpec(memory_space=smem),
        ],
        out_specs=pl.BlockSpec(memory_space=vmem),
        scratch_shapes=[
            vmem((64, 128, 128), f32),
            vmem((64, 128, 128), jnp.bfloat16),
            vmem((64, 128, 128), jnp.bfloat16),
            vmem((32, 128, 128), jnp.bfloat16),
            vmem((32, 128, 128), jnp.bfloat16),
            vmem((4, 4, 4, 128, 128), f32),
            vmem((4, 8), i32),
            vmem((8, 4, 64), i32),
            vmem((8, 128), i32),
            vmem((8, 8, 128), i32),
            vmem((8, 8, 128), i32),
            vmem((16, 8, 128), i32),
            smem((16, 8, 128), i32),
            smem((64,), i32),
            smem((64,), i32),
            smem((64,), f32),
            *[vmem((2, 4, 4, r, 128), f32) for r in rows],
            *[vmem((2, 4, 4, r, 128), f32) for r in rows],
            *[vmem((3, 4, r, 128), f32) for r in rows],
            *[vmem((4, 4, r, 128), f32) for r in rows],
            *[vmem((3, rows[n] + rows[n + 3], 128), f32) for n in range(3)],
            *[vmem((4, rows[n] + rows[n + 3], 128), f32) for n in range(3)],
            dma((3,)), dma((4,)), dma((7,)), dma((7,)), dma((7,)), dma((8,)), dma((7, 4)), dma((8, 4)),
            dma((4,)), dma((4,)), dma((1,)), dma((1,)), dma((6, 6)), dma((6, 6)), dma((6, 6)), dma((6, 6)),
        ],
        compiler_params=pltpu.CompilerParams(
            collective_id=0, has_side_effects=True, vmem_limit_bytes=40 << 20),
        cost_estimate=pl.CostEstimate(flops=64 * 3 * 2 * 128**3, bytes_accessed=1 << 22, transcendentals=0),
        name="home_product",
    )(*(pltpu.with_memory_space_constraint(a, pltpu.HBM) for a in (x_tiles, tile_col.T, keep_mask.transpose(0, 2, 1))), out_rows, out_cols)


def solution(mesh):
    return jax.shard_map(
        per_device,
        mesh=mesh,
        in_specs=(
            P("inner", "cols", None, None),
            P("inner", "cols"),
            P("inner", None, "cols"),
            P(("inner", "cols")),
            P(("inner", "cols")),
        ),
        out_specs=P(("inner", "cols"), None, None),
        check_vma=False,
    )
```

```python
import jax
import jax.numpy as jnp
from jax import lax
from jax.experimental import pallas as pl
from jax.experimental.pallas import tpu as pltpu
from jax.sharding import PartitionSpec as P

MESH = pl.DeviceIdType.MESH
JB_DEV = 60
PARTNERS = 16
STEPS = ((0, 1), (1, 0), (3, 0), (1, 1), (3, 1), (2, 0), (2, 1))
PARTS = ((0, 24, 16, (0, 1, 2)), (48, 24, 16, (1, 2, 0)), (88, 24, 16, (2, 0, 1)), (24, 24, 8, (0, 1, 2)), (72, 16, 8, (1, 2, 0)), (112, 16, 8, (2, 0, 1)))
HALVES = ((0, 1, 2), (3, 4, 5))


def kernel(x, tile_col_hbm, keep_hbm, out_row, out_col, out, held, left_top, left_low, right_top, right_low, products,
           tile_col, keep, mine, slots, notes, heard, heard_s, left_s, right_s, gate_s, *rest):
    vias, ones, twos, sums = (rest[6 * n:6 * n + 6] for n in range(4))
    threes, lines = rest[24:27], rest[27:30]
    (local_sem, own_sem, s_send, s_recv, n_send, n_recv, g_send, g_recv, c_send, c_recv, h_send, h_recv,
     f_send, f_recv, r_send, r_recv) = rest[30:]
    i = lax.axis_index("inner")
    c = lax.axis_index("cols")
    core = c % 2
    at = (i // 2, c // 4, (i % 2) * 2 + (c // 2) % 2)
    z_hi, z_lo = i % 2, (c // 2) % 2
    home = at[1] * 2 + z_lo

    def device(place, on):
        px, py, pz = place
        return (px * 2 + pz // 2, py * 4 + (pz % 2) * 2 + on)

    def row_home(step):
        py, pz = (at[1] + step[0]) % 4, (z_lo + step[1]) % 2
        return py * 2 + pz, device((at[0], py, z_hi * 2 + pz), core)

    def inner(e):
        return ((i + e) % 8, c)

    def along(axis, d):
        return device(tuple((p + d) % 4 if n == axis else p for n, p in enumerate(at)), core)

    twin = device(at, 1 - core)

    def remote(src, dst, send, recv, to):
        return pltpu.make_async_remote_copy(
            src_ref=src, dst_ref=dst, send_sem=send, recv_sem=recv, device_id=to, device_id_type=MESH)

    load_col = pltpu.make_async_copy(tile_col_hbm, tile_col, local_sem.at[0])
    load_keep = pltpu.make_async_copy(keep_hbm, keep, local_sem.at[1])
    load_col.start()
    load_keep.start()

    def load_own(p):
        return pltpu.make_async_copy(x.at[home, p], held.at[p * 8 + home], own_sem.at[p])

    for p in range(4):
        load_own(p).start()

    barrier = pltpu.get_barrier_semaphore()
    partners = [row_home(step)[1] for step in STEPS] + [inner(e) for e in range(1, 8)]
    partners += [twin, device((at[0], at[1], 3 - at[2]), core)]
    for to in partners:
        pl.semaphore_signal(barrier, inc=1, device_id=to, device_id_type=MESH)

    sublane = lax.broadcasted_iota(jnp.int32, (8, 128), 0)
    lane = lax.broadcasted_iota(jnp.int32, (8, 128), 1)
    mine[...] = jnp.where(sublane == 4, out_row[0], jnp.where(sublane == 5, out_col[0], 0))
    slots[i] = mine[...]
    load_col.wait()
    load_keep.wait()
    pl.semaphore_wait(barrier, PARTNERS)

    slot_copies = [remote(mine, slots.at[i], s_send.at[e - 1], s_recv.at[e - 1], inner(e)) for e in range(1, 8)]
    def send_blocks(p):
        for j, step in enumerate(STEPS):
            row, to = row_home(step)
            remote(x.at[row, p], held.at[p * 8 + home], g_send.at[j, p], g_recv.at[home, p], to).start()

    send_blocks(0)
    for copy in slot_copies:
        copy.start()
    send_blocks(1)
    for copy in slot_copies:
        copy.wait_recv()

    listed = jnp.zeros((8, 128), jnp.int32)
    for s in range(8):
        listed = jnp.where(lane == s, slots[s], listed)
    for k in range(8):
        notes[k] = listed
        notes[k, 0:4, 0:64] = keep[k]
        notes[k, 0:4, 64:128] = jnp.broadcast_to(tile_col[:, k:k + 1], (4, 64))
    heard[home] = notes[home]

    def note(j):
        row, to = row_home(STEPS[j])
        return remote(notes.at[row], heard.at[home], n_send.at[j], n_recv.at[home], to)

    for j in range(7):
        note(j).start()
    send_blocks(2)
    send_blocks(3)

    def share(p):
        return remote(held.at[pl.ds(p * 8, 8)], held.at[pl.ds(32 + p * 8, 8)], c_send.at[p], c_recv.at[p], twin)

    def halves(v):
        top = v.astype(jnp.bfloat16)
        return top, (v - top.astype(jnp.float32)).astype(jnp.bfloat16)

    def prepare_left(n):
        left_top[n], left_low[n] = halves(held[n].T)

    def receive(p):
        for j, step in enumerate(STEPS):
            source, to = row_home(step)
            remote(x.at[0, p], held.at[p * 8 + source], g_send.at[j, p], g_recv.at[source, p], to).wait_recv()
        load_own(p).wait()
        share(p).start()

        for n in range(p * 8, p * 8 + 8):
            prepare_left(n)
            right_top[n], right_low[n] = halves(held[n])

    def receive_shared(p):
        share(p).wait_recv()

        for n in range(p * 8, p * 8 + 8):
            prepare_left(32 + n)

    receive(0)
    receive(1)
    receive_shared(0)
    for j, step in enumerate(STEPS):
        source, to = row_home(step)
        remote(notes.at[0], heard.at[source], n_send.at[j], n_recv.at[source], to).wait_recv()
    share_notes = remote(heard.at[pl.ds(0, 8)], heard.at[pl.ds(8, 8)], h_send.at[0], h_recv.at[0], twin)
    share_notes.start()
    receive_shared(1)
    share_notes.wait_recv()
    stage = pltpu.make_async_copy(heard, heard_s, local_sem.at[2])
    stage.start()
    stage.wait()

    def find(n):
        sx, sy, sz = n // 16, (n // 4) % 4, n % 4
        index, chip = sx * 2 + sz // 2, sy * 2 + sz % 2
        row, col = heard_s[chip, 4, index], heard_s[chip, 5, index]
        left_slice = row // JB_DEV
        holder = jnp.where(left_slice % 2 == core, 0, 8) + left_slice // 2
        p, q, stored_l, stored_r = jnp.int32(0), jnp.int32(0), jnp.int32(0), jnp.int32(0)
        for r in range(4):
            hit = heard_s[holder, r, 64] == row
            p, stored_l = jnp.where(hit, r, p), jnp.where(hit, 1, stored_l)
            hit = heard_s[chip, r, 64] == col
            q, stored_r = jnp.where(hit, r, q), jnp.where(hit, 1, stored_r)
        left_s[n] = (holder // 8) * 32 + p * 8 + holder % 8
        right_s[n] = q * 8 + chip
        gate_s[n] = (heard_s[chip, q, left_slice * 4 + p] * stored_l * stored_r).astype(jnp.float32)

    def find_some(n, carry):
        for m in range(4):
            find(n * 4 + m)
        return carry

    lax.fori_loop(0, 16, find_some, 0)
    receive(2)
    receive_shared(2)
    receive(3)
    receive_shared(3)

    def product(n):
        lt, ll, rt, rl = left_top[left_s[n]], left_low[left_s[n]], right_top[right_s[n]], right_low[right_s[n]]
        return gate_s[n] * (jnp.dot(lt, rt, preferred_element_type=jnp.float32)
                            + jnp.dot(lt, rl, preferred_element_type=jnp.float32)
                            + jnp.dot(ll, rt, preferred_element_type=jnp.float32))

    def pick(axes_left, axis, where):
        return tuple(where if a == axis else slice(None) for a in axes_left)

    def first(part, way, kind):
        start, rows, split, (axis, _, _) = PARTS[part]
        ahead = 1 if way == 0 else 3
        low, high = (0, split), (split, rows - split)
        begin, count = (low if way == 0 else high) if kind != 1 else (high if way == 0 else low)
        if kind == 2:
            source = vias[part].at[way, :, :, pl.ds(begin, count)]
        else:
            cut = pick((0, 1, 2), axis, (at[axis] + (2 if kind == 0 else ahead)) % 4)
            source = products.at[cut + (pl.ds(start + begin, count),)]
        target = (vias if kind == 0 else ones)[part].at[way, :, :, pl.ds(begin, count)]
        n = way * 3 + kind
        return remote(source, target, f_send.at[part, n], f_recv.at[part, n], along(axis, ahead))

    def add_own(part, way):
        start, rows, split, (axis, _, _) = PARTS[part]
        first(part, way, 0).wait_recv()
        begin, count = (0, split) if way == 0 else (split, rows - split)

        cut = pick((0, 1, 2), axis, (at[axis] + 1 + 2 * way) % 4)
        free = [j for j, a in enumerate(cut) if isinstance(a, slice)]

        def body(n, carry):
            one = list(cut)
            one[free[0]] = n
            here = (way, n, slice(None), pl.ds(begin, count))
            vias[part][here] = vias[part][here] + products[tuple(one) + (pl.ds(start + begin, count),)]
            return carry

        lax.fori_loop(0, 4, body, 0)
        first(part, way, 2).start()

    def second(part, d):
        _, _, _, (gone, axis, _) = PARTS[part]
        cut = pick([a for a in range(3) if a != gone], axis, (at[axis] + d) % 4)
        return remote(sums[part].at[cut], twos[part].at[d - 1], r_send.at[part, d - 1], r_recv.at[part, d - 1], along(axis, d))

    def third(order, d):
        axis = PARTS[order][3][2]
        return remote(lines[order].at[(at[axis] + d) % 4], threes[order].at[d - 1],
                      r_send.at[order, 2 + d], r_recv.at[order, 2 + d], along(axis, d))

    def slab(j, carry):
        px = (at[0] + jnp.where(j < 2, 2 + j, 3 - j)) % 4

        for m in range(16):
            products[px, m // 4, m % 4] = product(px * 16 + m)

        @pl.when(j == 0)
        def _():
            for part in (0, 3):
                first(part, 0, 0).start()
                first(part, 1, 0).start()

        @pl.when(j == 1)
        def _():
            first(0, 1, 1).start()

        @pl.when(j == 2)
        def _():
            first(0, 0, 1).start()

        return carry

    lax.fori_loop(0, 4, slab, 0)
    def both_ways(part, kind):
        for way in range(2):
            first(part, way, kind).start()

    for part, kind in ((1, 0), (2, 0), (1, 1), (2, 1), (4, 0), (5, 0)):
        both_ways(part, kind)
    for copy in slot_copies + [share_notes]:
        copy.wait_send()
    for j, step in enumerate(STEPS):
        note(j).wait_send()
        row, to = row_home(step)
        for p in range(4):
            remote(x.at[row, p], held.at[p * 8 + home], g_send.at[j, p], g_recv.at[home, p], to).wait_send()
    for p in range(4):
        share(p).wait_send()
    for part in HALVES[0]:
        for way in range(2):
            add_own(part, way)
    for part in HALVES[1]:
        both_ways(part, 1)
    for part in HALVES[1]:
        for way in range(2):
            add_own(part, way)

    for part, (start, rows, _, (axis, _, _)) in enumerate(PARTS):
        for way in range(2):
            first(part, way, 1).wait_recv()
            first(part, way, 2).wait_recv()

        cut = pick((0, 1, 2), axis, at[axis])
        free = [j for j, a in enumerate(cut) if isinstance(a, slice)]

        def total(n, carry):
            one = list(cut)
            one[free[0]] = n
            sums[part][n] = products[tuple(one) + (pl.ds(start, rows),)] + ones[part][0, n] + ones[part][1, n]
            return carry

        lax.fori_loop(0, 4, total, 0)
        for d in (2, 1, 3):
            second(part, d).start()
    for part in range(6):
        for way in range(2):
            for kind in range(3):
                first(part, way, kind).wait_send()
    for part in (0, 3, 1, 4, 2, 5):
        _, rows, _, (gone, axis, _) = PARTS[part]
        order, inside = part % 3, (PARTS[part][0] - PARTS[part % 3][0])
        for d in range(1, 4):
            second(part, d).wait_recv()
        cut = pick([a for a in range(3) if a != gone], axis, at[axis])
        lines[order][:, pl.ds(inside, rows)] = sums[part][cut] + twos[part][0] + twos[part][1] + twos[part][2]
        if part > 2:
            for d in (2, 1, 3):
                third(order, d).start()
    for part in range(6):
        for d in range(1, 4):
            second(part, d).wait_send()
    for order in range(3):
        start, rows, axis = PARTS[order][0], PARTS[order][1] + PARTS[order + 3][1], PARTS[order][3][2]
        for d in range(1, 4):
            third(order, d).wait_recv()
        out[0, pl.ds(start, rows)] = lines[order][at[axis]] + threes[order][0] + threes[order][1] + threes[order][2]

    for order in range(3):
        for d in range(1, 4):
            third(order, d).wait_send()


def per_device(x_tiles, tile_col, keep_mask, out_rows, out_cols):
    vmem, smem = pltpu.VMEM, pltpu.SMEM
    dma = pltpu.SemaphoreType.DMA
    f32, i32 = jnp.float32, jnp.int32
    rows = [part[1] for part in PARTS]
    return pl.pallas_call(
        kernel,
        out_shape=jax.ShapeDtypeStruct((1, 128, 128), f32),
        in_specs=[
            pl.BlockSpec(memory_space=pltpu.HBM),
            pl.BlockSpec(memory_space=pltpu.HBM),
            pl.BlockSpec(memory_space=pltpu.HBM),
            pl.BlockSpec(memory_space=smem),
            pl.BlockSpec(memory_space=smem),
        ],
        out_specs=pl.BlockSpec(memory_space=vmem),
        scratch_shapes=[
            vmem((64, 128, 128), f32),
            vmem((64, 128, 128), jnp.bfloat16),
            vmem((64, 128, 128), jnp.bfloat16),
            vmem((32, 128, 128), jnp.bfloat16),
            vmem((32, 128, 128), jnp.bfloat16),
            vmem((4, 4, 4, 128, 128), f32),
            vmem((4, 8), i32),
            vmem((8, 4, 64), i32),
            vmem((8, 128), i32),
            vmem((8, 8, 128), i32),
            vmem((8, 8, 128), i32),
            vmem((16, 8, 128), i32),
            smem((16, 8, 128), i32),
            smem((64,), i32),
            smem((64,), i32),
            smem((64,), f32),
            *[vmem((2, 4, 4, r, 128), f32) for r in rows],
            *[vmem((2, 4, 4, r, 128), f32) for r in rows],
            *[vmem((3, 4, r, 128), f32) for r in rows],
            *[vmem((4, 4, r, 128), f32) for r in rows],
            *[vmem((3, rows[n] + rows[n + 3], 128), f32) for n in range(3)],
            *[vmem((4, rows[n] + rows[n + 3], 128), f32) for n in range(3)],
            dma((3,)), dma((4,)), dma((7,)), dma((7,)), dma((7,)), dma((8,)), dma((7, 4)), dma((8, 4)),
            dma((4,)), dma((4,)), dma((1,)), dma((1,)), dma((6, 6)), dma((6, 6)), dma((6, 6)), dma((6, 6)),
        ],
        compiler_params=pltpu.CompilerParams(
            collective_id=0, has_side_effects=True, vmem_limit_bytes=40 << 20),
        cost_estimate=pl.CostEstimate(flops=64 * 3 * 2 * 128**3, bytes_accessed=1 << 22, transcendentals=0),
        name="home_product",
    )(*(pltpu.with_memory_space_constraint(a, pltpu.HBM) for a in (x_tiles, tile_col.T, keep_mask.transpose(0, 2, 1))), out_rows, out_cols)


def solution(mesh):
    return jax.shard_map(
        per_device,
        mesh=mesh,
        in_specs=(
            P("inner", "cols", None, None),
            P("inner", "cols"),
            P("inner", None, "cols"),
            P(("inner", "cols")),
            P(("inner", "cols")),
        ),
        out_specs=P(("inner", "cols"), None, None),
        check_vma=False,
    )
```

```python
import jax
import jax.numpy as jnp
from jax import lax
from jax.experimental import pallas as pl
from jax.experimental.pallas import tpu as pltpu
from jax.sharding import PartitionSpec as P

MESH = pl.DeviceIdType.MESH
JB_DEV = 60
PARTNERS = 16
STEPS = ((0, 1), (1, 0), (3, 0), (1, 1), (3, 1), (2, 0), (2, 1))
PARTS = ((0, 24, 16, (0, 1, 2)), (48, 24, 16, (1, 2, 0)), (88, 24, 16, (2, 0, 1)), (24, 24, 8, (0, 1, 2)), (72, 16, 8, (1, 2, 0)), (112, 16, 8, (2, 0, 1)))
HALVES = ((0, 1, 2), (3, 4, 5))


def kernel(x, tile_col_hbm, keep_hbm, out_row, out_col, out, held, left_top, left_low, right_top, right_low, products,
           tile_col, keep, mine, slots, notes, heard, heard_s, left_s, right_s, gate_s, *rest):
    vias, ones, twos, sums = (rest[6 * n:6 * n + 6] for n in range(4))
    threes, lines = rest[24:27], rest[27:30]
    (local_sem, own_sem, s_send, s_recv, n_send, n_recv, g_send, g_recv, c_send, c_recv, h_send, h_recv,
     f_send, f_recv, r_send, r_recv) = rest[30:]
    i = lax.axis_index("inner")
    c = lax.axis_index("cols")
    core = c % 2
    at = (i // 2, c // 4, (i % 2) * 2 + (c // 2) % 2)
    z_hi, z_lo = i % 2, (c // 2) % 2
    home = at[1] * 2 + z_lo

    def device(place, on):
        px, py, pz = place
        return (px * 2 + pz // 2, py * 4 + (pz % 2) * 2 + on)

    def row_home(step):
        py, pz = (at[1] + step[0]) % 4, (z_lo + step[1]) % 2
        return py * 2 + pz, device((at[0], py, z_hi * 2 + pz), core)

    def inner(e):
        return ((i + e) % 8, c)

    def along(axis, d):
        return device(tuple((p + d) % 4 if n == axis else p for n, p in enumerate(at)), core)

    twin = device(at, 1 - core)

    def remote(src, dst, send, recv, to):
        return pltpu.make_async_remote_copy(
            src_ref=src, dst_ref=dst, send_sem=send, recv_sem=recv, device_id=to, device_id_type=MESH)

    load_col = pltpu.make_async_copy(tile_col_hbm, tile_col, local_sem.at[0])
    load_keep = pltpu.make_async_copy(keep_hbm, keep, local_sem.at[1])
    load_col.start()
    load_keep.start()

    def load_own(p):
        return pltpu.make_async_copy(x.at[home, p], held.at[p * 8 + home], own_sem.at[p])

    for p in range(4):
        load_own(p).start()

    barrier = pltpu.get_barrier_semaphore()
    partners = [row_home(step)[1] for step in STEPS] + [inner(e) for e in range(1, 8)]
    partners += [twin, device((at[0], at[1], 3 - at[2]), core)]
    for to in partners:
        pl.semaphore_signal(barrier, inc=1, device_id=to, device_id_type=MESH)

    sublane = lax.broadcasted_iota(jnp.int32, (8, 128), 0)
    lane = lax.broadcasted_iota(jnp.int32, (8, 128), 1)
    mine[...] = jnp.where(sublane == 4, out_row[0], jnp.where(sublane == 5, out_col[0], 0))
    slots[i] = mine[...]
    load_col.wait()
    load_keep.wait()
    pl.semaphore_wait(barrier, PARTNERS)

    slot_copies = [remote(mine, slots.at[i], s_send.at[e - 1], s_recv.at[e - 1], inner(e)) for e in range(1, 8)]
    def send_blocks(p):
        for j, step in enumerate(STEPS):
            row, to = row_home(step)
            remote(x.at[row, p], held.at[p * 8 + home], g_send.at[j, p], g_recv.at[home, p], to).start()

    send_blocks(0)
    for copy in slot_copies:
        copy.start()
    send_blocks(1)
    for copy in slot_copies:
        copy.wait_recv()

    listed = jnp.zeros((8, 128), jnp.int32)
    for s in range(8):
        listed = jnp.where(lane == s, slots[s], listed)
    for k in range(8):
        notes[k] = listed
        notes[k, 0:4, 0:64] = keep[k]
        notes[k, 0:4, 64:128] = jnp.broadcast_to(tile_col[:, k:k + 1], (4, 64))
    heard[home] = notes[home]

    def note(j):
        row, to = row_home(STEPS[j])
        return remote(notes.at[row], heard.at[home], n_send.at[j], n_recv.at[home], to)

    for j in range(7):
        note(j).start()
    send_blocks(2)
    send_blocks(3)

    def share(p):
        return remote(held.at[pl.ds(p * 8, 8)], held.at[pl.ds(32 + p * 8, 8)], c_send.at[p], c_recv.at[p], twin)

    def halves(v):
        top = v.astype(jnp.bfloat16)
        return top, (v - top.astype(jnp.float32)).astype(jnp.bfloat16)

    def prepare_left(n):
        left_top[n], left_low[n] = halves(held[n].T)

    def receive(p):
        for j, step in enumerate(STEPS):
            source, to = row_home(step)
            remote(x.at[0, p], held.at[p * 8 + source], g_send.at[j, p], g_recv.at[source, p], to).wait_recv()
        load_own(p).wait()
        share(p).start()

        for n in range(p * 8, p * 8 + 8):
            prepare_left(n)
            right_top[n], right_low[n] = halves(held[n])

    def receive_shared(p):
        share(p).wait_recv()

        for n in range(p * 8, p * 8 + 8):
            prepare_left(32 + n)

    receive(0)
    receive(1)
    receive_shared(0)
    for j, step in enumerate(STEPS):
        source, to = row_home(step)
        remote(notes.at[0], heard.at[source], n_send.at[j], n_recv.at[source], to).wait_recv()
    share_notes = remote(heard.at[pl.ds(0, 8)], heard.at[pl.ds(8, 8)], h_send.at[0], h_recv.at[0], twin)
    share_notes.start()
    receive_shared(1)
    share_notes.wait_recv()
    stage = pltpu.make_async_copy(heard, heard_s, local_sem.at[2])
    stage.start()
    stage.wait()

    def find(n):
        sx, sy, sz = n // 16, (n // 4) % 4, n % 4
        index, chip = sx * 2 + sz // 2, sy * 2 + sz % 2
        row, col = heard_s[chip, 4, index], heard_s[chip, 5, index]
        left_slice = row // JB_DEV
        holder = jnp.where(left_slice % 2 == core, 0, 8) + left_slice // 2
        p, q, stored_l, stored_r = jnp.int32(0), jnp.int32(0), jnp.int32(0), jnp.int32(0)
        for r in range(4):
            hit = heard_s[holder, r, 64] == row
            p, stored_l = jnp.where(hit, r, p), jnp.where(hit, 1, stored_l)
            hit = heard_s[chip, r, 64] == col
            q, stored_r = jnp.where(hit, r, q), jnp.where(hit, 1, stored_r)
        left_s[n] = (holder // 8) * 32 + p * 8 + holder % 8
        right_s[n] = q * 8 + chip
        gate_s[n] = (heard_s[chip, q, left_slice * 4 + p] * stored_l * stored_r).astype(jnp.float32)

    def find_some(n, carry):
        for m in range(4):
            find(n * 4 + m)
        return carry

    lax.fori_loop(0, 16, find_some, 0)
    receive(2)
    receive_shared(2)
    receive(3)
    receive_shared(3)

    def product(n):
        lt, ll, rt, rl = left_top[left_s[n]], left_low[left_s[n]], right_top[right_s[n]], right_low[right_s[n]]
        return gate_s[n] * (jnp.dot(lt, rt, preferred_element_type=jnp.float32)
                            + jnp.dot(lt, rl, preferred_element_type=jnp.float32)
                            + jnp.dot(ll, rt, preferred_element_type=jnp.float32))

    def pick(axes_left, axis, where):
        return tuple(where if a == axis else slice(None) for a in axes_left)

    def first(part, way, kind):
        start, rows, split, (axis, _, _) = PARTS[part]
        ahead = 1 if way == 0 else 3
        low, high = (0, split), (split, rows - split)
        begin, count = (low if way == 0 else high) if kind != 1 else (high if way == 0 else low)
        if kind == 2:
            source = vias[part].at[way, :, :, pl.ds(begin, count)]
        else:
            cut = pick((0, 1, 2), axis, (at[axis] + (2 if kind == 0 else ahead)) % 4)
            source = products.at[cut + (pl.ds(start + begin, count),)]
        target = (vias if kind == 0 else ones)[part].at[way, :, :, pl.ds(begin, count)]
        n = way * 3 + kind
        return remote(source, target, f_send.at[part, n], f_recv.at[part, n], along(axis, ahead))

    def add_own(part, way):
        start, rows, split, (axis, _, _) = PARTS[part]
        first(part, way, 0).wait_recv()
        begin, count = (0, split) if way == 0 else (split, rows - split)

        cut = pick((0, 1, 2), axis, (at[axis] + 1 + 2 * way) % 4)
        free = [j for j, a in enumerate(cut) if isinstance(a, slice)]

        def body(n, carry):
            one = list(cut)
            one[free[0]] = n
            here = (way, n, slice(None), pl.ds(begin, count))
            vias[part][here] = vias[part][here] + products[tuple(one) + (pl.ds(start + begin, count),)]
            return carry

        lax.fori_loop(0, 4, body, 0)
        first(part, way, 2).start()

    def second(part, d):
        _, _, _, (gone, axis, _) = PARTS[part]
        cut = pick([a for a in range(3) if a != gone], axis, (at[axis] + d) % 4)
        return remote(sums[part].at[cut], twos[part].at[d - 1], r_send.at[part, d - 1], r_recv.at[part, d - 1], along(axis, d))

    def third(order, d):
        axis = PARTS[order][3][2]
        return remote(lines[order].at[(at[axis] + d) % 4], threes[order].at[d - 1],
                      r_send.at[order, 2 + d], r_recv.at[order, 2 + d], along(axis, d))

    def slab(j, carry):
        px = (at[0] + jnp.where(j < 2, 2 + j, 3 - j)) % 4

        for m in range(16):
            products[px, m // 4, m % 4] = product(px * 16 + m)

        @pl.when(j == 0)
        def _():
            for part in (0, 3):
                first(part, 0, 0).start()
                first(part, 1, 0).start()

        @pl.when(j == 1)
        def _():
            first(0, 1, 1).start()

        @pl.when(j == 2)
        def _():
            first(0, 0, 1).start()

        return carry

    lax.fori_loop(0, 4, slab, 0)
    def both_ways(part, kind):
        for way in range(2):
            first(part, way, kind).start()

    for part, kind in ((1, 0), (2, 0), (1, 1), (2, 1), (4, 0), (5, 0)):
        both_ways(part, kind)
    for copy in slot_copies + [share_notes]:
        copy.wait_send()
    for j, step in enumerate(STEPS):
        note(j).wait_send()
        row, to = row_home(step)
        for p in range(4):
            remote(x.at[row, p], held.at[p * 8 + home], g_send.at[j, p], g_recv.at[home, p], to).wait_send()
    for p in range(4):
        share(p).wait_send()
    for part in HALVES[0]:
        for way in range(2):
            add_own(part, way)
    for part in HALVES[1]:
        both_ways(part, 1)
    for part in HALVES[1]:
        for way in range(2):
            add_own(part, way)

    for part, (start, rows, _, (axis, _, _)) in enumerate(PARTS):
        for way in range(2):
            first(part, way, 1).wait_recv()
            first(part, way, 2).wait_recv()

        cut = pick((0, 1, 2), axis, at[axis])
        free = [j for j, a in enumerate(cut) if isinstance(a, slice)]

        def total(n, carry):
            one = list(cut)
            one[free[0]] = n
            sums[part][n] = products[tuple(one) + (pl.ds(start, rows),)] + ones[part][0, n] + ones[part][1, n]
            return carry

        lax.fori_loop(0, 4, total, 0)
        for d in (2, 1, 3):
            second(part, d).start()
    for part in range(6):
        for way in range(2):
            for kind in range(3):
                first(part, way, kind).wait_send()
    for part in range(6):
        _, rows, _, (gone, axis, _) = PARTS[part]
        order, inside = part % 3, (PARTS[part][0] - PARTS[part % 3][0])
        for d in range(1, 4):
            second(part, d).wait_recv()
        cut = pick([a for a in range(3) if a != gone], axis, at[axis])
        lines[order][:, pl.ds(inside, rows)] = sums[part][cut] + twos[part][0] + twos[part][1] + twos[part][2]
        if part > 2:
            for d in (2, 1, 3):
                third(order, d).start()
    for part in range(6):
        for d in range(1, 4):
            second(part, d).wait_send()
    for order in range(3):
        start, rows, axis = PARTS[order][0], PARTS[order][1] + PARTS[order + 3][1], PARTS[order][3][2]
        for d in range(1, 4):
            third(order, d).wait_recv()
        out[0, pl.ds(start, rows)] = lines[order][at[axis]] + threes[order][0] + threes[order][1] + threes[order][2]

    for order in range(3):
        for d in range(1, 4):
            third(order, d).wait_send()


def per_device(x_tiles, tile_col, keep_mask, out_rows, out_cols):
    vmem, smem = pltpu.VMEM, pltpu.SMEM
    dma = pltpu.SemaphoreType.DMA
    f32, i32 = jnp.float32, jnp.int32
    rows = [part[1] for part in PARTS]
    return pl.pallas_call(
        kernel,
        out_shape=jax.ShapeDtypeStruct((1, 128, 128), f32),
        in_specs=[
            pl.BlockSpec(memory_space=pltpu.HBM),
            pl.BlockSpec(memory_space=pltpu.HBM),
            pl.BlockSpec(memory_space=pltpu.HBM),
            pl.BlockSpec(memory_space=smem),
            pl.BlockSpec(memory_space=smem),
        ],
        out_specs=pl.BlockSpec(memory_space=vmem),
        scratch_shapes=[
            vmem((64, 128, 128), f32),
            vmem((64, 128, 128), jnp.bfloat16),
            vmem((64, 128, 128), jnp.bfloat16),
            vmem((32, 128, 128), jnp.bfloat16),
            vmem((32, 128, 128), jnp.bfloat16),
            vmem((4, 4, 4, 128, 128), f32),
            vmem((4, 8), i32),
            vmem((8, 4, 64), i32),
            vmem((8, 128), i32),
            vmem((8, 8, 128), i32),
            vmem((8, 8, 128), i32),
            vmem((16, 8, 128), i32),
            smem((16, 8, 128), i32),
            smem((64,), i32),
            smem((64,), i32),
            smem((64,), f32),
            *[vmem((2, 4, 4, r, 128), f32) for r in rows],
            *[vmem((2, 4, 4, r, 128), f32) for r in rows],
            *[vmem((3, 4, r, 128), f32) for r in rows],
            *[vmem((4, 4, r, 128), f32) for r in rows],
            *[vmem((3, rows[n] + rows[n + 3], 128), f32) for n in range(3)],
            *[vmem((4, rows[n] + rows[n + 3], 128), f32) for n in range(3)],
            dma((3,)), dma((4,)), dma((7,)), dma((7,)), dma((7,)), dma((8,)), dma((7, 4)), dma((8, 4)),
            dma((4,)), dma((4,)), dma((1,)), dma((1,)), dma((6, 6)), dma((6, 6)), dma((6, 6)), dma((6, 6)),
        ],
        compiler_params=pltpu.CompilerParams(
            collective_id=0, has_side_effects=True, vmem_limit_bytes=40 << 20),
        cost_estimate=pl.CostEstimate(flops=64 * 3 * 2 * 128**3, bytes_accessed=1 << 22, transcendentals=0),
        name="home_product",
    )(*(pltpu.with_memory_space_constraint(a, pltpu.HBM) for a in (x_tiles, tile_col.T, keep_mask.transpose(0, 2, 1))), out_rows, out_cols)


def solution(mesh):
    return jax.shard_map(
        per_device,
        mesh=mesh,
        in_specs=(
            P("inner", "cols", None, None),
            P("inner", "cols"),
            P("inner", None, "cols"),
            P(("inner", "cols")),
            P(("inner", "cols")),
        ),
        out_specs=P(("inner", "cols"), None, None),
        check_vma=False,
    )
```
